128 devices in a mesh: row: 8 (over z, core), col: 16 (over y, x).
Axes of the slice: x: 4, y: 4, z: 4, core: 2. Of those that a mesh axis runs over, the one named last changes fastest.
Arguments:
- embeddings: bfloat16 [40960, 256], P(('row', 'col')), may hold values from -90 to 90
- start_vectors: float32 [32, 40960], P(None, ('row', 'col')), may hold values from -6 to 6
Outputs:
- vectors: float32 [32, 40960], P(None, ('row', 'col'))
- degrees: float32 [40960], P(('row', 'col'))
The draws below stay inside these ranges and needn't reach their ends.
All inputs are finite; a program needn't handle non-finite values.
Results may differ from the reference program's by a relative error of at most 0.015.
Values may be sent and summed in bfloat16 or wider, within the bound.
A program may use at most 128 MiB of HBM per device.

```python
import jax
import jax.numpy as jnp
from jax import lax

E = 256
K = 32
ITERS = 2
SPEAKERS = 64
NSEG = 40960
ROW_BLOCK = 5120


def draw_embeddings(key, part):
    key = jax.random.fold_in(key, 11)
    label_key, centre_key, strength_key, noise_key = jax.random.split(key, 4)
    labels = jax.random.randint(label_key, (NSEG,), 0, SPEAKERS)
    centres = jnp.clip(jax.random.normal(centre_key, (SPEAKERS, E), jnp.float32), -4.0, 4.0)
    strength = jax.random.uniform(strength_key, (NSEG, 1), jnp.float32, 0.6, 1.4)
    noise = 0.8 * jnp.clip(jax.random.normal(noise_key, (NSEG, E), jnp.float32), -4.0, 4.0)
    values = strength * jnp.take(centres, labels, axis=0) + noise
    return values.astype(jnp.bfloat16)


def block_levels(stream_key, shape, shards, least, top_value):
    def one(position, blocks):
        steps = jax.random.uniform(jax.random.fold_in(jax.random.fold_in(stream_key, 6), position), (blocks,), jnp.float32, least / len(shards), top_value / len(shards))
        return jnp.repeat(jnp.exp(steps), shape[position] // blocks).reshape((-1,) + (1,) * (len(shape) - position - 1))

    gain = one(*shards[0])
    for cut in shards[1:]:
        gain = gain * one(*cut)
    return gain


def normal_values(key, shape, spread, limit, cuts=(), kind=jnp.bfloat16):
    level = block_levels(key, shape, cuts, -0.22, 0.18) if cuts else 1.0
    result = jax.random.normal(key, shape, jnp.float32) * spread * level
    return jnp.minimum(jnp.maximum(result, -limit), limit).astype(kind)


def setup_inputs(seed: int = 0) -> dict:
    key_list = jax.random.split(jax.random.key(seed), 3)
    return {
        "embeddings": draw_embeddings(jax.random.fold_in(key_list[2], 71), 0),
        "start_vectors": normal_values(key_list[1], (K, NSEG), 1.0, 6.0, ((1, 128),), jnp.float32),
    }


def normalize(embeddings):
    values = embeddings.astype(jnp.float32)
    power = lax.optimization_barrier(jnp.mean(values * values, axis=1, keepdims=True))
    return (values * lax.rsqrt(power + 1e-06) / jnp.sqrt(jnp.float32(E))).astype(jnp.bfloat16)

def affinity_block(left, right):
    inner = jnp.dot(left.astype(jnp.float32), right.astype(jnp.float32).T, precision=lax.Precision.HIGHEST)
    return jnp.exp(8.0 * (inner - 1.0)).astype(jnp.bfloat16)

def reference(embeddings, start_vectors):
    unit = normalize(embeddings)
    blocks = NSEG // ROW_BLOCK
    unit_blocks = unit.reshape(blocks, ROW_BLOCK, E)

    def degree_of(block):
        return lax.optimization_barrier(jnp.sum(affinity_block(block, unit).astype(jnp.float32), axis=1))
    degrees = lax.map(degree_of, unit_blocks).reshape(NSEG)
    scale = 1.0 / jnp.sqrt(degrees)
    current = start_vectors
    for step in range(ITERS):
        scaled = (current * scale[None, :]).astype(jnp.bfloat16).astype(jnp.float32)

        def apply_block(block):
            tile = affinity_block(block, unit).astype(jnp.float32)
            return jnp.dot(scaled, tile.T, precision=lax.Precision.HIGHEST)
        image = lax.map(apply_block, unit_blocks)
        image = jnp.transpose(image, (1, 0, 2)).reshape(K, NSEG) * scale[None, :]
        gram = jnp.dot(image, image.T, precision=lax.Precision.HIGHEST)
        lower = jnp.linalg.cholesky(gram)
        current = lax.linalg.triangular_solve(lower, image, left_side=True, lower=True)
    return (current, degrees)
```

```python
import functools
import math

import jax
import jax.numpy as jnp
from jax import lax
from jax.experimental import pallas as pl
from jax.experimental.pallas import tpu as pltpu
from jax.sharding import PartitionSpec as P

ITERS = 2
K = 32
E = 256
OWN = 320
NB = 128
NA = OWN - NB
NZ = 8
NQ = 4
J = NZ * OWN
RATE = 8.0 / math.log(2.0)
MESH = pl.DeviceIdType.MESH
HIGH = lax.Precision.HIGHEST
F32 = jnp.float32
BF16 = jnp.bfloat16


def dot_nt(a, b, precision=None):
    return lax.dot_general(a, b, (((1,), (1,)), ((), ())), precision=precision, preferred_element_type=F32)


def pack(square):
    return jnp.concatenate([square[8 * b : 8 * b + 8, :] for b in range(4)], axis=1)


def unpack(packed):
    return jnp.concatenate([packed[:, K * b : K * b + K] for b in range(4)], axis=0)


def inverse_factor(gram):
    rows = lax.broadcasted_iota(jnp.int32, (K, K), 0)
    columns = lax.broadcasted_iota(jnp.int32, (K, K), 1)
    eye = (rows == columns).astype(F32)
    work = jnp.concatenate([gram, eye], axis=1)
    below = lax.broadcasted_iota(jnp.int32, (K, 1), 0)
    pivots = jnp.ones((K, 1), F32)
    for k in range(K):
        pivot = work[k : k + 1, k : k + 1]
        column = work[:, k : k + 1]
        factor = jnp.where(below > k, column / pivot, 0.0)
        pivots = jnp.where(below == k, pivot, pivots)
        work = work - factor * work[k : k + 1, :]
    return work[:, K : 2 * K] * (1.0 / jnp.sqrt(pivots))


def kernel(
    emb_ref, start_ref, vec_ref, deg_ref,
    u_a, u_b, u_j, t_a, t_b, acc, start_all, part_send, part_recv, scale_all,
    lhs, send_a, send_b, recv_a, recv_b, raw_all, gram_z, gram_xy, image_ref,
    s_a, r_a, s_b, r_b, s_z, r_z, s_st, r_st, s_pt, r_pt, s_pa, r_pa, s_pb, r_pb, s_rw, r_rw, s_gz, r_gz, s_gx, r_gx,
):
    row = lax.axis_index("row")
    col = lax.axis_index("col")
    z, core = row // 2, row % 2
    x, y = col % NQ, col // NQ
    p = x + core * (y - x)
    q = y + core * (x - y)

    def at_pq(dp, dq):
        pp = lax.rem(p + dp + NQ, NQ)
        qq = lax.rem(q + dq + NQ, NQ)
        return (row, qq * (4 - 3 * core) + pp * (1 + 3 * core))

    def at_z(dz, dc):
        return (lax.rem(z + dz + NQ, NQ) * 2 + lax.rem(core + dc, 2), col)

    offsets_xy = [(dp, dq) for dq in range(NQ) for dp in range(NQ) if dp or dq]
    offsets_z = [(dz, dc) for dz in range(NQ) for dc in range(2) if dz or dc]
    sends = []

    def push(src, dst, s_sem, r_sem, device):
        copy = pltpu.make_async_remote_copy(
            src_ref=src, dst_ref=dst, send_sem=s_sem, recv_sem=r_sem, device_id=device, device_id_type=MESH
        )
        copy.start()
        sends.append(copy)

    def arrived(dst, s_sem, r_sem):
        pltpu.make_async_remote_copy(
            src_ref=dst, dst_ref=dst, send_sem=s_sem, recv_sem=r_sem, device_id=(row, col), device_id_type=MESH
        ).wait_recv()

    barrier = pltpu.get_barrier_semaphore()
    for dp, dq in offsets_xy:
        pl.semaphore_signal(barrier, inc=1, device_id=at_pq(dp, dq), device_id_type=MESH)
    for dz, dc in offsets_z:
        pl.semaphore_signal(barrier, inc=1, device_id=at_z(dz, dc), device_id_type=MESH)

    values = emb_ref[...].astype(F32)
    power = jnp.mean(values * values, axis=1, keepdims=True)
    unit = (values * lax.rsqrt(power + 1e-06) * (1.0 / math.sqrt(E))).astype(BF16)
    u_b[0, 0:NB, :] = unit[0:NB]
    u_a[0, 0:NA, :] = unit[NB:OWN]
    u_j[row] = unit
    start_all[row] = start_ref[...]
    acc[...] = jnp.zeros_like(acc)
    pl.semaphore_wait(barrier, len(offsets_xy) + len(offsets_z))

    def slot_a(dq, dp):
        return u_a.at[dq, pl.ds(dp * NA, NA)]

    def slot_b(dp, dq):
        return u_b.at[dp, pl.ds(dq * NB, NB)]

    def push_piece_a(dp):
        for dq in (1, 3):
            push(slot_a(0, dp), slot_a(dq, dp), s_a.at[dq, dp, 0], r_a.at[dq, dp, 0], at_pq(0, dq))

    def push_piece_b(dq):
        for dp in (1, 3):
            push(slot_b(0, dq), slot_b(dp, dq), s_b.at[dp, dq, 0], r_b.at[dp, dq, 0], at_pq(dp, 0))

    push(u_j.at[row], u_j.at[row], s_z.at[0, 1], r_z.at[0, 1], at_z(0, 1))
    for dz in (1, 3, 2):
        push(u_j.at[row], u_j.at[row], s_z.at[dz, 0], r_z.at[dz, 0], at_z(dz, 0))
    for d in (1, 3, 2):
        push(slot_a(0, 0), slot_a(0, d), s_a.at[0, d, 0], r_a.at[0, d, 0], at_pq(d, 0))
        push(slot_b(0, 0), slot_b(0, d), s_b.at[0, d, 0], r_b.at[0, d, 0], at_pq(0, d))
    push_piece_a(0)
    push_piece_b(0)

    def shard(dz, dc):
        return lax.rem(z - dz + NQ, NQ) * 2 + lax.rem(core + dc, 2)

    for d in (1, 3, 2):
        arrived(slot_a(0, d), s_a.at[0, d, 0], r_a.at[0, d, 0])
        push_piece_a(d)
        arrived(slot_b(0, d), s_b.at[0, d, 0], r_b.at[0, d, 0])
        push_piece_b(d)

    def tile(u_ref, t_ref, chunk, owner):
        rows_j = pl.ds(pl.multiple_of(owner * OWN, OWN), OWN)
        value = jnp.exp2(dot_nt(u_j[owner], u_ref[chunk]) * RATE)
        t_ref[chunk, rows_j, :] = value.astype(BF16)
        total = acc[rows_j, :]
        for lane in range(0, u_ref.shape[1], 128):
            total = total + value[:, lane : lane + 128]
        acc[rows_j, :] = total

    def tile_both(chunk, owner):
        tile(u_a, t_a, chunk, owner)
        tile(u_b, t_b, chunk, owner)

    def first(dz):
        def body(dc, carry):
            tile_both(0, shard(dz, dc))
            return carry

        lax.fori_loop(0, 2, body, 0)

    arrived(u_j.at[shard(0, 1)], s_z.at[0, 1], r_z.at[0, 1])
    first(0)
    for dz in (1, 3, 2):
        source = shard(dz, 0)
        arrived(u_j.at[source], s_z.at[dz, 0], r_z.at[dz, 0])
        push(u_j.at[source], u_j.at[source], s_z.at[dz, 1], r_z.at[dz, 1], at_z(0, 1))
        if dz == 2:
            for dz2, dc2 in offsets_z:
                push(start_all.at[row], start_all.at[row], s_st.at[dz2, dc2], r_st.at[dz2, dc2], at_z(dz2, dc2))
        arrived(u_j.at[shard(dz, 1)], s_z.at[dz, 1], r_z.at[dz, 1])
        first(dz)

    for d in range(NQ):
        for step, half in ((1, 0), (3, 1)):
            rows_a = pl.ds(d * NA + half * (NA // 2), NA // 2)
            rows_b = pl.ds(d * NB + half * (NB // 2), NB // 2)
            arrived(slot_a(step, d), s_a.at[step, d, 0], r_a.at[step, d, 0])
            push(u_a.at[step, rows_a], u_a.at[2, rows_a], s_a.at[2, d, half], r_a.at[2, d, half], at_pq(0, step))
            arrived(slot_b(step, d), s_b.at[step, d, 0], r_b.at[step, d, 0])
            push(u_b.at[step, rows_b], u_b.at[2, rows_b], s_b.at[2, d, half], r_b.at[2, d, half], at_pq(step, 0))

    def rest(chunk):
        def body(owner, carry):
            tile_both(chunk, owner)
            return carry

        lax.fori_loop(0, NZ, body, 0)

    rest(1)
    rest(3)
    for d in range(NQ):
        for half in range(2):
            rows_a = pl.ds(d * NA + half * (NA // 2), NA // 2)
            rows_b = pl.ds(d * NB + half * (NB // 2), NB // 2)
            arrived(u_a.at[2, rows_a], s_a.at[2, d, half], r_a.at[2, d, half])
            arrived(u_b.at[2, rows_b], s_b.at[2, d, half], r_b.at[2, d, half])
    rest(2)

    ones = jnp.ones((8, 128), BF16)
    for owner in range(NZ):
        rest_f32 = acc[owner * OWN : (owner + 1) * OWN, :]
        total = jnp.zeros((8, OWN), F32)
        for _ in range(3):
            piece = rest_f32.astype(BF16)
            rest_f32 = rest_f32 - piece.astype(F32)
            total = total + dot_nt(ones, piece)
        part_send[owner : owner + 1, :] = total[0:1, :]
    for dz, dc in offsets_z:
        push(part_send, part_recv.at[dz, dc], s_pt.at[dz, dc], r_pt.at[dz, dc], at_z(dz, dc))
    for dz, dc in offsets_z:
        arrived(start_all.at[shard(dz, dc)], s_st.at[dz, dc], r_st.at[dz, dc])
    for dz, dc in offsets_z:
        arrived(part_recv.at[dz, dc], s_pt.at[dz, dc], r_pt.at[dz, dc])
    degrees = part_send[...]
    for dz, dc in offsets_z:
        degrees = degrees + part_recv[dz, dc]
    part_recv[0, 0] = degrees
    scales = 1.0 / jnp.sqrt(degrees)
    scale_all[...] = scales
    deg_ref[...] = part_recv[0, 0, pl.ds(row, 1), :] * math.exp(-8.0)
    scale = scale_all[pl.ds(row, 1), :]

    for owner in range(NZ):
        lhs[:, owner * OWN : (owner + 1) * OWN] = (start_all[owner] * scales[owner : owner + 1, :]).astype(BF16)

    for step in range(ITERS):
        for chunk in (2, 1, 3, 0):
            out = jnp.dot(lhs[...], t_a[chunk], preferred_element_type=F32)
            for dp in range(NQ):
                block = out[:, dp * NA : (dp + 1) * NA]
                if dp or chunk:
                    send_a[step, chunk, dp] = block.astype(BF16)
                    push(send_a.at[step, chunk, dp], recv_a.at[step, chunk, dp], s_pa.at[step, chunk, dp],
                         r_pa.at[step, chunk, dp], at_pq(-dp, -chunk))
                else:
                    image_ref[:, NB:OWN] = block
            out = jnp.dot(lhs[...], t_b[chunk], preferred_element_type=F32)
            for dq in range(NQ):
                block = out[:, dq * NB : (dq + 1) * NB]
                if dq or chunk:
                    send_b[step, chunk, dq] = block.astype(BF16)
                    push(send_b.at[step, chunk, dq], recv_b.at[step, chunk, dq], s_pb.at[step, chunk, dq],
                         r_pb.at[step, chunk, dq], at_pq(-chunk, -dq))
                else:
                    image_ref[:, 0:NB] = block
        total_a = image_ref[:, NB:OWN]
        total_b = image_ref[:, 0:NB]
        for chunk in (2, 1, 3, 0):
            for d in range(NQ):
                if d or chunk:
                    arrived(recv_a.at[step, chunk, d], s_pa.at[step, chunk, d], r_pa.at[step, chunk, d])
                    total_a = total_a + recv_a[step, chunk, d].astype(F32)
                    arrived(recv_b.at[step, chunk, d], s_pb.at[step, chunk, d], r_pb.at[step, chunk, d])
                    total_b = total_b + recv_b[step, chunk, d].astype(F32)
        image_ref[:, NB:OWN] = total_a
        image_ref[:, 0:NB] = total_b
        image = image_ref[...] * scale
        gram = pack(dot_nt(image, image, HIGH))
        gram_z[step, 0, 0] = gram
        for dz, dc in offsets_z:
            push(gram_z.at[step, 0, 0], gram_z.at[step, dz, dc], s_gz.at[step, dz, dc], r_gz.at[step, dz, dc], at_z(dz, dc))
        if step + 1 < ITERS:
            raw_all[row] = image * scale
            for dz, dc in offsets_z:
                push(raw_all.at[row], raw_all.at[row], s_rw.at[dz, dc], r_rw.at[dz, dc], at_z(dz, dc))
        for dz, dc in offsets_z:
            arrived(gram_z.at[step, dz, dc], s_gz.at[step, dz, dc], r_gz.at[step, dz, dc])
            gram = gram + gram_z[step, dz, dc]
        gram_xy[step, 0, 0] = gram
        for dp, dq in offsets_xy:
            push(gram_xy.at[step, 0, 0], gram_xy.at[step, dq, dp], s_gx.at[step, dq, dp], r_gx.at[step, dq, dp], at_pq(dp, dq))
        for dp, dq in offsets_xy:
            arrived(gram_xy.at[step, dq, dp], s_gx.at[step, dq, dp], r_gx.at[step, dq, dp])
            gram = gram + gram_xy[step, dq, dp]
        inverse = inverse_factor(unpack(gram))
        if step + 1 < ITERS:
            for dz, dc in offsets_z:
                arrived(raw_all.at[shard(dz, dc)], s_rw.at[dz, dc], r_rw.at[dz, dc])
            for owner in range(NZ):
                lhs[:, owner * OWN : (owner + 1) * OWN] = jnp.dot(
                    inverse, raw_all[owner], precision=HIGH, preferred_element_type=F32
                ).astype(BF16)
        else:
            vec_ref[...] = jnp.dot(inverse, image, precision=HIGH, preferred_element_type=F32)

    for copy in sends:
        copy.wait_send()


def local(embeddings, start_vectors):
    dma = pltpu.SemaphoreType.DMA
    vmem = pltpu.VMEM
    pairs = []
    for shape in (
        (NQ, NQ, 2), (NQ, NQ, 2), (NQ, 2), (NQ, 2), (NQ, 2), (ITERS, NQ, NQ), (ITERS, NQ, NQ), (NQ, 2),
        (ITERS, NQ, 2), (ITERS, NQ, NQ),
    ):
        pairs += [dma(shape), dma(shape)]
    vectors, degrees = pl.pallas_call(
        kernel,
        out_shape=(jax.ShapeDtypeStruct((K, OWN), F32), jax.ShapeDtypeStruct((1, OWN), F32)),
        in_specs=[pl.BlockSpec(memory_space=vmem)] * 2,
        out_specs=(pl.BlockSpec(memory_space=vmem), pl.BlockSpec(memory_space=vmem)),
        scratch_shapes=[
            vmem((NQ, NQ * NA, E), BF16),
            vmem((NQ, NQ * NB, E), BF16),
            vmem((NZ, OWN, E), BF16),
            vmem((NQ, J, NQ * NA), BF16),
            vmem((NQ, J, NQ * NB), BF16),
            vmem((J, 128), F32),
            vmem((NZ, K, OWN), F32),
            vmem((NZ, OWN), F32),
            vmem((NQ, 2, NZ, OWN), F32),
            vmem((NZ, OWN), F32),
            vmem((K, J), BF16),
            vmem((ITERS, NQ, NQ, K, NA), BF16),
            vmem((ITERS, NQ, NQ, K, NB), BF16),
            vmem((ITERS, NQ, NQ, K, NA), BF16),
            vmem((ITERS, NQ, NQ, K, NB), BF16),
            vmem((NZ, K, OWN), F32),
            vmem((ITERS, NQ, 2, 8, 128), F32),
            vmem((ITERS, NQ, NQ, 8, 128), F32),
            vmem((K, OWN), F32),
            *pairs,
        ],
        compiler_params=pltpu.CompilerParams(
            collective_id=0, has_side_effects=True, vmem_limit_bytes=56 * 2**20
        ),
        name="subspace",
    )(embeddings, start_vectors)
    return (vectors, degrees.reshape(OWN))


def solution(mesh):
    return jax.shard_map(
        local,
        mesh=mesh,
        in_specs=(P(("row", "col"), None), P(None, ("row", "col"))),
        out_specs=(P(None, ("row", "col")), P(("row", "col"))),
        check_vma=False,
    )
```

```python
import math

import jax
import jax.numpy as jnp
from jax import lax
from jax.experimental import pallas as pl
from jax.experimental.pallas import tpu as pltpu
from jax.sharding import PartitionSpec as P

K = 32
E = 256
OWN = 320
HALF = OWN // 2
NZ = 8
NQ = 4
J = NZ * OWN
PAIR = 2 * OWN
WIDE = NQ * OWN
RATE = 8.0 / math.log(2.0)
MESH = pl.DeviceIdType.MESH
HIGH = lax.Precision.HIGHEST
F32 = jnp.float32
BF16 = jnp.bfloat16
ORDER = (
    (0, 0), (1, 0), (3, 0), (0, 1),
    (0, 3), (2, 0), (0, 2), (1, 1),
    (1, 3), (3, 1), (3, 3), (1, 2),
    (3, 2), (2, 1), (2, 3), (2, 2),
)
SLOT = {place: slot for slot, place in enumerate(ORDER)}


def dot_nt(a, b, precision=None):
    return lax.dot_general(a, b, (((1,), (1,)), ((), ())), precision=precision, preferred_element_type=F32)


def pack(square):
    return jnp.concatenate([square[8 * b : 8 * b + 8, :] for b in range(4)], axis=1)


def unpack(packed):
    return jnp.concatenate([packed[:, K * b : K * b + K] for b in range(4)], axis=0)


def inverse_factor(gram):
    rows = lax.broadcasted_iota(jnp.int32, (K, K), 0)
    columns = lax.broadcasted_iota(jnp.int32, (K, K), 1)
    eye = (rows == columns).astype(F32)
    work = jnp.concatenate([gram, eye], axis=1)
    below = lax.broadcasted_iota(jnp.int32, (K, 1), 0)
    pivots = jnp.ones((K, 1), F32)
    for k in range(K):
        pivot = work[k : k + 1, k : k + 1]
        column = work[:, k : k + 1]
        factor = jnp.where(below > k, column / pivot, 0.0)
        pivots = jnp.where(below == k, pivot, pivots)
        work = work - factor * work[k : k + 1, :]
    return work[:, K : 2 * K] * (1.0 / jnp.sqrt(pivots))


def kernel(
    emb_ref, start_ref, vec_ref, deg_ref,
    u_i, u_j, tiles, acc, start_all, part, scale_all, lhs, lhs_pair, out_acc,
    send_1, recv_1, send_2, recv_2, raw_all, gram_z, gram_xy,
    s_i, r_i, s_j, r_j, s_st, r_st, s_pt, r_pt, s_1, r_1, s_2, r_2, s_rw, r_rw, s_gz, r_gz, s_gx, r_gx,
):
    row = lax.axis_index("row")
    col = lax.axis_index("col")
    z, core = row // 2, row % 2
    x, y = col % NQ, col // NQ
    p = x + core * (y - x)
    q = y + core * (x - y)

    def at_pq(dp, dq):
        pp = lax.rem(p + dp + NQ, NQ)
        qq = lax.rem(q + dq + NQ, NQ)
        return (row, qq * (4 - 3 * core) + pp * (1 + 3 * core))

    def shard(dz, dc):
        return lax.rem(z - dz + NQ, NQ) * 2 + lax.rem(core + dc, 2)

    def at_z(dz, dc):
        return (shard(-dz % NQ, dc), col)

    offsets_z = [(dz, dc) for dz in range(NQ) for dc in range(2) if dz or dc]
    sibling = at_z(0, 1)

    def push(src, dst, s_sem, r_sem, device):
        pltpu.make_async_remote_copy(
            src_ref=src, dst_ref=dst, send_sem=s_sem, recv_sem=r_sem, device_id=device, device_id_type=MESH
        ).start()

    def arrived(ref, r_sem):
        pltpu.make_async_remote_copy(
            src_ref=ref, dst_ref=ref, send_sem=r_sem, recv_sem=r_sem, device_id=sibling, device_id_type=MESH
        ).wait_recv()

    def sent(ref, s_sem):
        pltpu.make_async_remote_copy(
            src_ref=ref, dst_ref=ref, send_sem=s_sem, recv_sem=s_sem, device_id=sibling, device_id_type=MESH
        ).wait_send()

    barrier = pltpu.get_barrier_semaphore()
    neighbours = [at_pq(1, 0), at_pq(3, 0), at_pq(0, 1), at_pq(0, 3), at_z(1, 0), at_z(3, 0), sibling]
    for device in neighbours:
        pl.semaphore_signal(barrier, inc=1, device_id=device, device_id_type=MESH)

    values = emb_ref[...].astype(F32)
    power = jnp.mean(values * values, axis=1, keepdims=True)
    unit = (values * lax.rsqrt(power + 1e-06) * (1.0 / math.sqrt(E))).astype(BF16)
    u_i[0] = unit
    u_j[row] = unit
    start_all[row] = start_ref[...]
    acc[...] = jnp.zeros_like(acc)
    pl.semaphore_wait(barrier, len(neighbours))

    def piece(source, target, device):
        push(u_i.at[SLOT[source]], u_i.at[SLOT[target]], s_i, r_i.at[SLOT[target]], device)

    def half_piece(source, target, half, device):
        rows = pl.ds(half * HALF, HALF)
        push(u_i.at[SLOT[source], rows], u_i.at[SLOT[target], rows], s_i, r_i.at[SLOT[target]], device)

    def here(place):
        arrived(u_i.at[SLOT[place]], r_i.at[SLOT[place]])

    def second_ring(d):
        piece((d, 0), (d, 1), at_pq(0, 1))
        piece((d, 0), (d, 3), at_pq(0, 3))

    def on_first(d):
        here((d, 0))
        half_piece((d, 0), (2, 0), 0 if d == 1 else 1, at_pq(d, 0))
        second_ring(d)

    def on_second(d, e):
        here((d, e))
        half_piece((d, e), (d, 2), 0 if e == 1 else 1, at_pq(0, e))

    def shard_push(dz, device, sem):
        push(u_j.at[shard(dz, 0)], u_j.at[shard(dz, 0)], s_j, sem, device)

    def on_z(dz):
        source = shard(dz, 0)
        arrived(u_j.at[source], r_j.at[dz, 0])
        shard_push(dz, sibling, r_j.at[dz, 1])
        if dz != 2:
            rows = pl.ds(0 if dz == 1 else HALF, HALF)
            push(u_j.at[source, rows], u_j.at[source, rows], s_j, r_j.at[2, 0], at_z(dz, 0))

    def tile(chunk, owner):
        rows_j = pl.ds(pl.multiple_of(owner * OWN, OWN), OWN)
        block = u_i[NQ * chunk : NQ * chunk + NQ].reshape(WIDE, E)
        value = jnp.exp2(dot_nt(u_j[owner], block) * RATE)
        tiles[chunk, rows_j, :] = value.astype(BF16)
        total = acc[rows_j, :]
        for lane in range(0, WIDE, 128):
            total = total + value[:, lane : lane + 128]
        acc[rows_j, :] = total

    def tile_pair(chunk, dz):
        arrived(u_j.at[shard(dz, 1)], r_j.at[dz, 1])

        def body(dc, carry):
            tile(chunk, shard(dz, dc))
            return carry

        lax.fori_loop(0, 2, body, 0)

    def tile_range(chunk, first, last):
        def body(owner, carry):
            tile(chunk, owner)
            return carry

        lax.fori_loop(first, last, body, 0)

    shard_push(0, sibling, r_j.at[0, 1])
    piece((0, 0), (1, 0), at_pq(1, 0))
    piece((0, 0), (3, 0), at_pq(3, 0))
    shard_push(0, at_z(1, 0), r_j.at[1, 0])
    shard_push(0, at_z(3, 0), r_j.at[3, 0])
    second_ring(0)
    on_first(1)
    on_first(3)
    on_second(0, 1)
    on_second(0, 3)
    on_z(1)
    on_z(3)
    tile_pair(0, 0)
    tile_pair(0, 1)
    here((2, 0))
    second_ring(2)
    tile_pair(0, 3)
    on_second(1, 1)
    on_second(1, 3)
    on_z(2)
    for dz, dc in offsets_z:
        push(start_all.at[row], start_all.at[row], s_st, r_st, at_z(dz, dc))
    tile_pair(0, 2)
    on_second(3, 1)
    on_second(3, 3)
    here((0, 2))
    tile_range(1, 0, NZ // 2)
    on_second(2, 1)
    on_second(2, 3)
    tile_range(1, NZ // 2, NZ)
    here((1, 2))
    tile_range(2, 0, NZ)
    here((3, 2))
    here((2, 2))
    tile_range(3, 0, NZ)
    arrived(start_all.at[0:7], r_st)

    ones = jnp.ones((8, 128), BF16)
    for owner in range(NZ):
        left = acc[owner * OWN : (owner + 1) * OWN, :]
        total = jnp.zeros((8, OWN), F32)
        for _ in range(3):
            top = left.astype(BF16)
            left = left - top.astype(F32)
            total = total + dot_nt(ones, top)
        part[0, owner : owner + 1, :] = total[0:1, :]
    for dz, dc in offsets_z:
        push(part.at[0], part.at[2 * dz + dc], s_pt, r_pt, at_z(dz, dc))
    arrived(part.at[1:8], r_pt)
    degrees = part[0]
    for slot in range(1, NZ):
        degrees = degrees + part[slot]
    scales = 1.0 / jnp.sqrt(degrees)
    scale_all[0] = scales
    scale_all[1] = degrees * math.exp(-8.0)
    deg_ref[...] = scale_all[1, pl.ds(row, 1), :]
    scale = scale_all[0, pl.ds(row, 1), :]
    for owner in range(NZ):
        lhs[:, owner * OWN : (owner + 1) * OWN] = (start_all[owner] * scales[owner : owner + 1, :]).astype(BF16)

    def scatter(chunk, out, send, recv, s_sem, r_sem):
        for sub in range(NQ):
            slot = NQ * chunk + sub
            block = out[:, sub * OWN : (sub + 1) * OWN]
            if slot == 0:
                return_own = block
                continue
            send[slot] = block.astype(send.dtype)
            dp, dq = ORDER[slot]
            push(send.at[slot], recv.at[slot], s_sem, r_sem, at_pq(-dp, -dq))
        return return_own if chunk == 0 else None

    def gathered(own, recv, r_sem):
        arrived(recv.at[1:16], r_sem)
        for slot in range(1, NQ * NQ):
            own = own + recv[slot].astype(F32)
        return own * scale

    for chunk in (3, 2, 1, 0):
        own = scatter(chunk, jnp.dot(lhs[...], tiles[chunk], preferred_element_type=F32), send_1, recv_1, s_1, r_1)
    image = gathered(own, recv_1, r_1)

    raw = image * scale
    high = raw.astype(BF16)
    raw_all[row, 0:K, :] = high
    raw_all[row, K : 2 * K, :] = (raw - high.astype(F32)).astype(BF16)

    def raw_push(dz, device, sem):
        push(raw_all.at[shard(dz, 0)], raw_all.at[shard(dz, 0)], s_rw, sem, device)

    raw_push(0, sibling, r_rw.at[0, 1])
    for dz in (2, 1, 3):
        raw_push(0, at_z(dz, 0), r_rw.at[dz, 0])

    def gram_start(step, image):
        gram_z[step, 0] = pack(dot_nt(image, image, HIGH))
        for dz, dc in offsets_z:
            push(gram_z.at[step, 0], gram_z.at[step, 2 * dz + dc], s_gz.at[step], r_gz.at[step], at_z(dz, dc))

    def gram_middle(step):
        arrived(gram_z.at[step, 1:8], r_gz.at[step])
        gram = gram_z[step, 0]
        for slot in range(1, NZ):
            gram = gram + gram_z[step, slot]
        gram_xy[step, 0] = gram
        for slot in range(1, NQ * NQ):
            dp, dq = ORDER[slot]
            push(gram_xy.at[step, 0], gram_xy.at[step, slot], s_gx.at[step], r_gx.at[step], at_pq(dp, dq))

    def gram_end(step):
        arrived(gram_xy.at[step, 1:16], r_gx.at[step])
        gram = gram_xy[step, 0]
        for slot in range(1, NQ * NQ):
            gram = gram + gram_xy[step, slot]
        return inverse_factor(unpack(gram))

    gram_start(0, image)

    def product(dz, chunk):
        first = lax.rem(z - dz + NQ, NQ) * 2
        rows = pl.ds(pl.multiple_of(first * OWN, PAIR), PAIR)
        out = jnp.dot(lhs_pair[...], tiles[chunk, rows, :], preferred_element_type=F32)
        return out[0:K] + out[K : 2 * K]

    for dz in (0, 1, 3, 2):
        first = lax.rem(z - dz + NQ, NQ) * 2
        if dz:
            arrived(raw_all.at[shard(dz, 0)], r_rw.at[dz, 0])
            raw_push(dz, sibling, r_rw.at[dz, 1])
        if dz == 1:
            gram_middle(0)
        arrived(raw_all.at[shard(dz, 1)], r_rw.at[dz, 1])
        lhs_pair[:, 0:OWN] = raw_all[first]
        lhs_pair[:, OWN:PAIR] = raw_all[first + 1]
        for chunk in (3, 2, 1, 0):
            out = product(dz, chunk)
            if dz == 0:
                out_acc[chunk] = out
            elif dz != 2:
                out_acc[chunk] += out
            else:
                own = scatter(chunk, out_acc[chunk] + out, send_2, recv_2, s_2, r_2)
    inverse = gram_end(0)
    image = gathered(own, recv_2, r_2)
    image = jnp.dot(inverse, image, precision=HIGH, preferred_element_type=F32)
    gram_start(1, image)
    gram_middle(1)
    inverse = gram_end(1)
    vec_ref[...] = jnp.dot(inverse, image, precision=HIGH, preferred_element_type=F32)

    sent(u_i.at[0:15], s_i)
    sent(u_j.at[0:7], s_j)
    sent(start_all.at[0:7], s_st)
    sent(part.at[1:8], s_pt)
    sent(send_1.at[1:16], s_1)
    sent(raw_all.at[0:7], s_rw)
    sent(send_2.at[1:16], s_2)
    for step in range(2):
        sent(gram_z.at[step, 1:8], s_gz.at[step])
        sent(gram_xy.at[step, 1:16], s_gx.at[step])


def local(embeddings, start_vectors):
    dma = pltpu.SemaphoreType.DMA
    vmem = pltpu.VMEM
    vectors, degrees = pl.pallas_call(
        kernel,
        out_shape=(jax.ShapeDtypeStruct((K, OWN), F32), jax.ShapeDtypeStruct((1, OWN), F32)),
        in_specs=[pl.BlockSpec(memory_space=vmem)] * 2,
        out_specs=(pl.BlockSpec(memory_space=vmem), pl.BlockSpec(memory_space=vmem)),
        scratch_shapes=[
            vmem((NQ * NQ, OWN, E), BF16),
            vmem((NZ, OWN, E), BF16),
            vmem((NQ, J, WIDE), BF16),
            vmem((J, 128), F32),
            vmem((NZ, K, OWN), F32),
            vmem((NZ, NZ, OWN), F32),
            vmem((2, NZ, OWN), F32),
            vmem((K, J), BF16),
            vmem((2 * K, PAIR), BF16),
            vmem((NQ, K, WIDE), F32),
            vmem((NQ * NQ, K, OWN), BF16),
            vmem((NQ * NQ, K, OWN), BF16),
            vmem((NQ * NQ, K, OWN), F32),
            vmem((NQ * NQ, K, OWN), F32),
            vmem((NZ, 2 * K, OWN), BF16),
            vmem((2, NZ, 8, 128), F32),
            vmem((2, NQ * NQ, 8, 128), F32),
            dma, dma((NQ * NQ,)),
            dma, dma((NQ, 2)),
            dma, dma,
            dma, dma,
            dma, dma,
            dma, dma,
            dma, dma((NQ, 2)),
            dma((2,)), dma((2,)),
            dma((2,)), dma((2,)),
        ],
        compiler_params=pltpu.CompilerParams(
            collective_id=0, has_side_effects=True, vmem_limit_bytes=56 * 2**20
        ),
        name="subspace",
    )(embeddings, start_vectors)
    return (vectors, degrees.reshape(OWN))


def solution(mesh):
    return jax.shard_map(
        local,
        mesh=mesh,
        in_specs=(P(("row", "col"), None), P(None, ("row", "col"))),
        out_specs=(P(None, ("row", "col")), P(("row", "col"))),
        check_vma=False,
    )
```

```python
import math

import jax
import jax.numpy as jnp
from jax import lax
from jax.experimental import pallas as pl
from jax.experimental.pallas import tpu as pltpu
from jax.sharding import PartitionSpec as P

K = 32
PLACES = ((0, 0), (0, 1), (1, 0), (3, 0), (2, 0), (1, 1), (3, 1), (2, 1))
E = 256
OWN = 320
HALF = OWN // 2
NZ = 8
NQ = 4
J = NZ * OWN
PAIR = 2 * OWN
WIDE = NQ * OWN
RATE = 8.0 / math.log(2.0)
MESH = pl.DeviceIdType.MESH
HIGH = lax.Precision.HIGHEST
F32 = jnp.float32
BF16 = jnp.bfloat16


def dot_nt(a, b, precision=None):
    return lax.dot_general(a, b, (((1,), (1,)), ((), ())), precision=precision, preferred_element_type=F32)


def pack(square):
    return jnp.concatenate([square[8 * b : 8 * b + 8, :] for b in range(4)], axis=1)


def unpack(packed):
    return jnp.concatenate([packed[:, K * b : K * b + K] for b in range(4)], axis=0)


def inverse_factor(gram):
    rows = lax.broadcasted_iota(jnp.int32, (K, K), 0)
    columns = lax.broadcasted_iota(jnp.int32, (K, K), 1)
    eye = (rows == columns).astype(F32)
    work = jnp.concatenate([gram, eye], axis=1)
    below = lax.broadcasted_iota(jnp.int32, (K, 1), 0)
    pivots = jnp.ones((K, 1), F32)
    for k in range(K):
        pivot = work[k : k + 1, k : k + 1]
        column = work[:, k : k + 1]
        factor = jnp.where(below > k, column / pivot, 0.0)
        pivots = jnp.where(below == k, pivot, pivots)
        work = work - factor * work[k : k + 1, :]
    return work[:, K : 2 * K] * (1.0 / jnp.sqrt(pivots))


def kernel(
    emb_ref, start_ref, vec_ref, deg_ref,
    u_i, u_j, tiles, acc, start_all, part, scale_all, lhs, lhs_pair, out_acc,
    sib_send, sib_recv, sum_send, sum_recv, raw_all, gram_c, gram_r,
    s_i, r_i, s_j, r_j, s_st, r_st, s_pt, r_pt, s_sb, r_sb, s_sm, r_sm, s_rw, r_rw, s_gc, r_gc, s_gr, r_gr,
):
    row = lax.axis_index("row")
    col = lax.axis_index("col")
    z, core = row // 2, row % 2
    x, y = col % NQ, col // NQ
    y_rows = y + 1 - 2 * (y % 2)
    y_cols = NQ - 1 - y
    sibling = (z * 2 + 1 - core, col)

    def at_r(dx, dy, dc=0):
        place = (y_rows if dy else y) * NQ + lax.rem(x + dx + NQ, NQ)
        return (z * 2 + (1 - core if dc else core), place)

    def at_c(dz, dy):
        return (lax.rem(z + dz + NQ, NQ) * 2 + core, (y_cols if dy else y) * NQ + x)

    def j_slot(dz, dy):
        return lax.rem(z - dz + NQ, NQ) * 2 + (y // 2) + dy * (1 - 2 * (y // 2))

    offsets_c = [(dz, dy) for dz, dy in PLACES if dz or dy]
    offsets_r = [(dx, dy, dc) for dx, dy in PLACES for dc in range(2) if dx or dy or dc]
    mine = j_slot(0, 0)

    def push(src, dst, s_sem, r_sem, device):
        pltpu.make_async_remote_copy(
            src_ref=src, dst_ref=dst, send_sem=s_sem, recv_sem=r_sem, device_id=device, device_id_type=MESH
        ).start()

    def arrived(ref, r_sem):
        pltpu.make_async_remote_copy(
            src_ref=ref, dst_ref=ref, send_sem=r_sem, recv_sem=r_sem, device_id=sibling, device_id_type=MESH
        ).wait_recv()

    def sent(ref, s_sem):
        pltpu.make_async_remote_copy(
            src_ref=ref, dst_ref=ref, send_sem=s_sem, recv_sem=s_sem, device_id=sibling, device_id_type=MESH
        ).wait_send()

    barrier = pltpu.get_barrier_semaphore()
    neighbours = [at_r(1, 0), at_r(3, 0), at_r(0, 1), at_c(1, 0), at_c(3, 0), at_c(0, 1), sibling]
    for device in neighbours:
        pl.semaphore_signal(barrier, inc=1, device_id=device, device_id_type=MESH)

    values = emb_ref[...].astype(F32)
    power = jnp.mean(values * values, axis=1, keepdims=True)
    unit = (values * lax.rsqrt(power + 1e-06) * (1.0 / math.sqrt(E))).astype(BF16)
    u_i[0] = unit
    u_j[mine] = unit
    start_all[mine] = start_ref[...]
    acc[...] = jnp.zeros_like(acc)
    pl.semaphore_wait(barrier, len(neighbours))

    def i_slot(dx, dy, dc=0):
        return 2 * PLACES.index((dx % NQ, dy)) + dc

    def row_piece(dx, dy, step, flip, half=None):
        rows = pl.ds(0, OWN) if half is None else pl.ds(half * HALF, HALF)
        to = i_slot(dx + step, dy ^ flip)
        push(u_i.at[i_slot(dx, dy), rows], u_i.at[to, rows], s_i, r_i.at[to], at_r(step, flip))

    def row_over(dx, dy):
        push(u_i.at[i_slot(dx, dy)], u_i.at[i_slot(dx, dy, 1)], s_i, r_i.at[i_slot(dx, dy, 1)], sibling)

    def row_here(dx, dy, dc=0):
        arrived(u_i.at[i_slot(dx, dy, dc)], r_i.at[i_slot(dx, dy, dc)])

    def col_piece(dz, dy, step, flip, half=None):
        rows = pl.ds(0, OWN) if half is None else pl.ds(half * HALF, HALF)
        slot = j_slot(dz, dy)
        push(u_j.at[slot, rows], u_j.at[slot, rows], s_j, r_j.at[(dz + step) % NQ, dy ^ flip], at_c(step, flip))

    def col_over(dz, dy):
        pass

    def col_here(dz, dy):
        arrived(u_j.at[j_slot(dz, dy)], r_j.at[dz, dy])

    def event(here, piece, over, d, dy):
        here(d, dy)
        if d in (1, 3) and dy == 0:
            piece(d, 0, d, 0, 0 if d == 1 else 1)
            pl.when(core == 1)(lambda: piece(d, 0, 0, 1))
        elif (d, dy) == (0, 1):

            @pl.when(core == 0)
            def _():
                piece(0, 1, 1, 0)
                piece(0, 1, 3, 0)

        elif (d, dy) == (2, 0):
            pl.when(core == 1)(lambda: piece(2, 0, 0, 1))
        elif d in (1, 3):
            pl.when(core == 0)(lambda: piece(d, 1, d, 0, 0 if d == 1 else 1))
        over(d, dy)

    def on_row(dx, dy):
        event(row_here, row_piece, row_over, dx, dy)

    def on_col(dz, dy):
        event(col_here, col_piece, col_over, dz, dy)

    def tile(chunk, slot):
        rows_j = pl.ds(pl.multiple_of(slot * OWN, OWN), OWN)
        block = u_i[pl.ds(NQ * chunk, NQ)].reshape(WIDE, E)
        value = jnp.exp2(dot_nt(u_j[slot], block) * RATE)
        tiles[chunk, rows_j, :] = value.astype(BF16)
        total = acc[rows_j, :]
        for lane in range(0, WIDE, 128):
            total = total + value[:, lane : lane + 128]
        acc[rows_j, :] = total

    def tile_range(first, last, count, place):
        def body(n, carry):
            tile(first + lax.rem(n, last - first), j_slot(*place(n // (last - first))))
            return carry

        lax.fori_loop(0, count * (last - first), body, 0)

    def near(n):
        return (n // 2) * (2 * (n % 2) + 1), (1 - n // 2) * (n % 2)

    def beside(n):
        return 2 * n + 1, 1

    row_over(0, 0)
    for piece in (row_piece, col_piece):
        piece(0, 0, 0, 1)
        piece(0, 0, 1, 0)
        piece(0, 0, 3, 0)
    for place in PLACES[1:4]:
        on_row(*place)
        on_col(*place)
    for dx, dy in PLACES[0:2]:
        row_here(dx, dy, 1)
    tile_range(0, 1, 4, near)
    for dx, dy in PLACES[2:4]:
        row_here(dx, dy, 1)
    on_row(2, 0)
    on_col(2, 0)
    tile_range(1, 2, 4, near)
    for place in PLACES[5:7]:
        on_row(*place)
        on_col(*place)
    tile_range(0, 2, 2, beside)
    row_here(2, 0, 1)
    row_here(1, 1, 1)
    tile_range(2, 3, 4, near)
    on_col(2, 1)
    for dz, dy in offsets_c:
        push(start_all.at[mine], start_all.at[mine], s_st, r_st, at_c(dz, dy))
    on_row(2, 1)
    tile_range(2, 3, 2, beside)
    row_here(3, 1, 1)
    row_here(2, 1, 1)
    tile_range(3, 4, 4, near)
    tile_range(3, 4, 2, beside)
    tile_range(0, 4, 2, lambda n: (2, n))
    arrived(start_all.at[0:7], r_st)

    ones = jnp.ones((8, 128), BF16)
    for slot in range(NZ):
        left = acc[slot * OWN : (slot + 1) * OWN, :]
        total = jnp.zeros((8, OWN), F32)
        for _ in range(3):
            top = left.astype(BF16)
            left = left - top.astype(F32)
            total = total + dot_nt(ones, top)
        part[0, slot : slot + 1, :] = total[0:1, :]
    for n, (dz, dy) in enumerate(offsets_c):
        push(part.at[0], part.at[n + 1], s_pt, r_pt, at_c(dz, dy))
    arrived(part.at[1:8], r_pt)
    degrees = part[0]
    for n in range(1, NZ):
        degrees = degrees + part[n]
    scales = 1.0 / jnp.sqrt(degrees)
    scale_all[0] = scales
    scale_all[1] = degrees * math.exp(-8.0)
    deg_ref[...] = scale_all[1, pl.ds(mine, 1), :]
    scale = scale_all[0, pl.ds(mine, 1), :]
    for slot in range(NZ):
        lhs[:, slot * OWN : (slot + 1) * OWN] = (start_all[slot] * scales[slot : slot + 1, :]).astype(BF16)

    def to_sibling(step, chunk, out):
        pair = pl.ds(2 * chunk, 2)
        for sub in range(2):
            sum_send[step, 2 * chunk + sub] = out[:, sub * PAIR : sub * PAIR + OWN]
            sib_send[step, 2 * chunk + sub] = out[:, sub * PAIR + OWN : (sub + 1) * PAIR]
        push(sib_send.at[step, pair], sib_recv.at[step, pair], s_sb.at[step], r_sb.at[step, chunk], sibling)

    def to_owners(step, chunk):
        arrived(sib_recv.at[step, pl.ds(2 * chunk, 2)], r_sb.at[step, chunk])
        for n in (2 * chunk + 1, 2 * chunk):
            dx, dy = PLACES[n]
            sum_send[step, n] += sib_recv[step, n]
            if n:
                push(sum_send.at[step, n], sum_recv.at[step, n], s_sm.at[step], r_sm.at[step], at_r(-dx, dy))

    def gathered(step):
        arrived(sum_recv.at[step, 1:8], r_sm.at[step])
        total = sum_send[step, 0]
        for n in range(1, NZ):
            total = total + sum_recv[step, n]
        return total * scale

    for chunk in (3, 2, 1, 0):
        to_sibling(0, chunk, jnp.dot(lhs[...], tiles[chunk], preferred_element_type=F32))
        if chunk < 3:
            to_owners(0, chunk + 1)
    to_owners(0, 0)
    image = gathered(0)

    raw = image * scale
    high = raw.astype(BF16)
    raw_all[mine, 0:K, :] = high
    raw_all[mine, K : 2 * K, :] = (raw - high.astype(F32)).astype(BF16)
    for dz, dy in ((0, 1), (1, 1), (3, 1), (2, 1), (2, 0), (1, 0), (3, 0)):
        push(raw_all.at[mine], raw_all.at[mine], s_rw, r_rw.at[dz, dy], at_c(dz, dy))

    def gram_start(step, image):
        gram_c[step, 0] = pack(dot_nt(image, image, HIGH))
        for n, (dz, dy) in enumerate(offsets_c):
            push(gram_c.at[step, 0], gram_c.at[step, n + 1], s_gc.at[step], r_gc.at[step], at_c(dz, dy))

    def gram_middle(step):
        arrived(gram_c.at[step, 1:8], r_gc.at[step])
        gram = gram_c[step, 0]
        for n in range(1, NZ):
            gram = gram + gram_c[step, n]
        gram_r[step, 0] = gram
        for n, (dx, dy, dc) in enumerate(offsets_r):
            push(gram_r.at[step, 0], gram_r.at[step, n + 1], s_gr.at[step], r_gr.at[step], at_r(dx, dy, dc))

    def gram_end(step):
        arrived(gram_r.at[step, 1:16], r_gr.at[step])
        gram = gram_r[step, 0]
        for n in range(1, 2 * NZ):
            gram = gram + gram_r[step, n]
        return inverse_factor(unpack(gram))

    gram_start(0, image)

    def product(dz, chunk):
        rows = pl.ds(pl.multiple_of(lax.rem(z - dz + NQ, NQ) * PAIR, PAIR), PAIR)
        out = jnp.dot(lhs_pair[dz], tiles[chunk, rows, :], preferred_element_type=F32)
        return out[0:K] + out[K : 2 * K]

    def ready(dz):
        first = lax.rem(z - dz + NQ, NQ) * 2
        for dy in range(2):
            if dz or dy:
                arrived(raw_all.at[j_slot(dz, dy)], r_rw.at[dz, dy])
        lhs_pair[dz, :, 0:OWN] = raw_all[first]
        lhs_pair[dz, :, OWN:PAIR] = raw_all[first + 1]

    ready(0)
    for chunk in range(4):
        out_acc[chunk] = product(0, chunk)
    ready(1)
    ready(3)
    for chunk in (3, 2):
        out_acc[chunk] += product(1, chunk) + product(3, chunk)
    gram_middle(0)
    ready(2)
    for chunk in (3, 2):
        to_sibling(1, chunk, out_acc[chunk] + product(2, chunk))
    to_owners(1, 3)
    for chunk in (1, 0):
        to_sibling(1, chunk, out_acc[chunk] + product(1, chunk) + product(3, chunk) + product(2, chunk))
        to_owners(1, chunk + 1)
    to_owners(1, 0)
    inverse = gram_end(0)
    image = gathered(1)
    image = jnp.dot(inverse, image, precision=HIGH, preferred_element_type=F32)
    gram_start(1, image)
    gram_middle(1)
    inverse = gram_end(1)
    vec_ref[...] = jnp.dot(inverse, image, precision=HIGH, preferred_element_type=F32)

    sent(u_i.at[0:15], s_i)
    sent(u_j.at[0:7], s_j)
    sent(start_all.at[0:7], s_st)
    sent(part.at[1:8], s_pt)
    sent(raw_all.at[0:7], s_rw)
    for step in range(2):
        sent(sib_send.at[step], s_sb.at[step])
        sent(sum_send.at[step, 1:8], s_sm.at[step])
        sent(gram_c.at[step, 1:8], s_gc.at[step])
        sent(gram_r.at[step, 1:16], s_gr.at[step])


def local(embeddings, start_vectors):
    dma = pltpu.SemaphoreType.DMA
    vmem = pltpu.VMEM
    vectors, degrees = pl.pallas_call(
        kernel,
        out_shape=(jax.ShapeDtypeStruct((K, OWN), F32), jax.ShapeDtypeStruct((1, OWN), F32)),
        in_specs=[pl.BlockSpec(memory_space=vmem)] * 2,
        out_specs=(pl.BlockSpec(memory_space=vmem), pl.BlockSpec(memory_space=vmem)),
        scratch_shapes=[
            vmem((NQ * NQ, OWN, E), BF16),
            vmem((NZ, OWN, E), BF16),
            vmem((NQ, J, WIDE), BF16),
            vmem((J, 128), F32),
            vmem((NZ, K, OWN), F32),
            vmem((NZ, NZ, OWN), F32),
            vmem((2, NZ, OWN), F32),
            vmem((K, J), BF16),
            vmem((NQ, 2 * K, PAIR), BF16),
            vmem((NQ, K, WIDE), F32),
            vmem((2, NZ, K, OWN), F32),
            vmem((2, NZ, K, OWN), F32),
            vmem((2, NZ, K, OWN), F32),
            vmem((2, NZ, K, OWN), F32),
            vmem((NZ, 2 * K, OWN), BF16),
            vmem((2, NZ, 8, 128), F32),
            vmem((2, 2 * NZ, 8, 128), F32),
            dma, dma((2 * NZ,)),
            dma, dma((NQ, 2)),
            dma, dma,
            dma, dma,
            dma((2,)), dma((2, NQ)),
            dma((2,)), dma((2,)),
            dma, dma((NQ, 2)),
            dma((2,)), dma((2,)),
            dma((2,)), dma((2,)),
        ],
        compiler_params=pltpu.CompilerParams(
            collective_id=0, has_side_effects=True, vmem_limit_bytes=56 * 2**20
        ),
        name="subspace",
    )(embeddings, start_vectors)
    return (vectors, degrees.reshape(OWN))


def solution(mesh):
    return jax.shard_map(
        local,
        mesh=mesh,
        in_specs=(P(("row", "col"), None), P(None, ("row", "col"))),
        out_specs=(P(None, ("row", "col")), P(("row", "col"))),
        check_vma=False,
    )
```

```python
import math

import jax
import jax.numpy as jnp
from jax import lax
from jax.experimental import pallas as pl
from jax.experimental.pallas import tpu as pltpu
from jax.sharding import PartitionSpec as P

K = 32
PLACES = ((0, 0), (0, 1), (1, 0), (3, 0), (2, 0), (1, 1), (3, 1), (2, 1))
E = 256
OWN = 320
PAD = 384
NZ = 8
NQ = 4
J = NZ * OWN
PAIR = 2 * OWN
WIDE = NQ * OWN
RATE = 8.0 / math.log(2.0)
MESH = pl.DeviceIdType.MESH
HIGH = lax.Precision.HIGHEST
F32 = jnp.float32
BF16 = jnp.bfloat16


def dot_nt(a, b, precision=None):
    return lax.dot_general(a, b, (((1,), (1,)), ((), ())), precision=precision, preferred_element_type=F32)


def pack(square):
    return jnp.concatenate([square[8 * b : 8 * b + 8, :] for b in range(4)], axis=1)


def unpack(packed):
    return jnp.concatenate([packed[:, K * b : K * b + K] for b in range(4)], axis=0)


def inverse_factor(gram):
    shape = (8, 2 * K)
    ranks = lax.broadcasted_iota(jnp.int32, (8, K), 0)
    lanes = lax.broadcasted_iota(jnp.int32, (8, K), 1)
    rank = lax.broadcasted_iota(jnp.int32, shape, 0)
    work = [
        jnp.concatenate([gram[8 * b : 8 * b + 8], (lanes == ranks + 8 * b).astype(F32)], axis=1) for b in range(4)
    ]
    done = []
    for b in range(4):
        rows = [jnp.broadcast_to(work[b][i : i + 1], shape) for i in range(8)]
        columns = [
            [jnp.broadcast_to(work[c][:, 8 * b + i : 8 * b + i + 1], shape) for c in range(b, 4)] for i in range(8)
        ]
        corner = [[jnp.broadcast_to(columns[j][0][i : i + 1], shape) for j in range(i + 1)] for i in range(8)]
        pivots = corner[0][0]
        for i in range(8):
            pivots = jnp.where(rank == i, corner[i][i], pivots)
            inverse = 1.0 / corner[i][i]
            factors = [column * inverse for column in columns[i]]
            factors[0] = jnp.where(rank > i, factors[0], 0.0)
            for j in range(i + 1, 8):
                factor = corner[j][i] * inverse
                rows[j] = rows[j] - factor * rows[i]
                columns[j] = [old - own * corner[j][i] for old, own in zip(columns[j], factors)]
                for k in range(i + 1, j + 1):
                    corner[j][k] = corner[j][k] - factor * corner[k][i]
            for c in range(b, 4):
                work[c] = work[c] - factors[c - b] * rows[i]
        done.append(work[b] * (1.0 / jnp.sqrt(pivots)))
    return jnp.concatenate(done, axis=0)[:, K : 2 * K]


def kernel(
    emb_ref, start_ref, vec_ref, deg_ref,
    u_i, u_j, tiles, acc, start_all, part, scale_all, lhs, lhs_pair, out_acc,
    sib_send, sib_recv, sum_send, sum_recv, raw_all, gram_c, gram_r,
    s_i, r_i, s_j, r_j, s_st, r_st, s_pt, r_pt, s_sb, r_sb, s_sm, r_sm, s_rw, r_rw, s_gc, r_gc, s_gr, r_gr,
):
    row = lax.axis_index("row")
    col = lax.axis_index("col")
    z, core = row // 2, row % 2
    x, y = col % NQ, col // NQ
    y_rows = y + 1 - 2 * (y % 2)
    y_cols = NQ - 1 - y
    sibling = (z * 2 + 1 - core, col)

    def at_r(dx, dy, dc=0):
        place = (y_rows if dy else y) * NQ + lax.rem(x + dx + NQ, NQ)
        return (z * 2 + (1 - core if dc else core), place)

    def at_c(dz, dy):
        return (lax.rem(z + dz + NQ, NQ) * 2 + core, (y_cols if dy else y) * NQ + x)

    def j_slot(dz, dy):
        return lax.rem(z - dz + NQ, NQ) * 2 + (y // 2) + dy * (1 - 2 * (y // 2))

    offsets_c = [(dz, dy) for dz, dy in PLACES if dz or dy]
    offsets_r = [(dx, dy, dc) for dx, dy in PLACES for dc in range(2) if dx or dy or dc]
    mine = j_slot(0, 0)

    def push(src, dst, s_sem, r_sem, device):
        pltpu.make_async_remote_copy(
            src_ref=src, dst_ref=dst, send_sem=s_sem, recv_sem=r_sem, device_id=device, device_id_type=MESH
        ).start()

    def arrived(ref, r_sem):
        pltpu.make_async_remote_copy(
            src_ref=ref, dst_ref=ref, send_sem=r_sem, recv_sem=r_sem, device_id=sibling, device_id_type=MESH
        ).wait_recv()

    def sent(ref, s_sem):
        pltpu.make_async_remote_copy(
            src_ref=ref, dst_ref=ref, send_sem=s_sem, recv_sem=s_sem, device_id=sibling, device_id_type=MESH
        ).wait_send()

    barrier = pltpu.get_barrier_semaphore()
    neighbours = [at_r(*place) for place in PLACES[1:5]] + [at_c(*place) for place in PLACES[1:]] + [sibling]
    for device in neighbours:
        pl.semaphore_signal(barrier, inc=1, device_id=device, device_id_type=MESH)

    values = emb_ref[...].astype(F32)
    power = jnp.mean(values * values, axis=1, keepdims=True)
    unit = (values * lax.rsqrt(power + 1e-06) * (1.0 / math.sqrt(E))).astype(BF16)
    u_i[0] = unit
    u_j[mine] = unit
    start_all[mine, :, 0:OWN] = start_ref[...]
    acc[...] = jnp.zeros_like(acc)
    pl.semaphore_wait(barrier, len(neighbours))

    def i_slot(dx, dy, dc=0):
        return 2 * PLACES.index((dx % NQ, dy)) + dc

    def row_piece(dx, dy, step, flip):
        to = i_slot(dx + step, dy ^ flip)
        push(u_i.at[i_slot(dx, dy)], u_i.at[to], s_i, r_i.at[to], at_r(step, flip))

    def row_over(dx, dy):
        push(u_i.at[i_slot(dx, dy)], u_i.at[i_slot(dx, dy, 1)], s_i, r_i.at[i_slot(dx, dy, 1)], sibling)

    def row_here(dx, dy, dc=0):
        arrived(u_i.at[i_slot(dx, dy, dc)], r_i.at[i_slot(dx, dy, dc)])

    def col_piece(dz, dy, step, flip):
        slot = j_slot(dz, dy)
        push(u_j.at[slot], u_j.at[slot], s_j, r_j.at[(dz + step) % NQ, dy ^ flip], at_c(step, flip))

    def col_here(dz, dy):
        arrived(u_j.at[j_slot(dz, dy)], r_j.at[dz, dy])

    def onward(piece, d, dy):
        if (d, dy) == (0, 1):

            @pl.when(core == 0)
            def _():
                for step in (1, 3, 2):
                    piece(0, 1, step, 0)

        elif dy == 0:
            pl.when(core == 1)(lambda: piece(d, 0, 0, 1))

    def on_row(dx, dy):
        row_here(dx, dy)
        onward(row_piece, dx, dy)
        row_over(dx, dy)

    def on_col(dz, dy):
        col_here(dz, dy)
        onward(col_piece, dz, dy)

    def tile(chunk, slot, low=0, high=WIDE):
        rows_j = pl.ds(pl.multiple_of(slot * OWN, OWN), OWN)
        block = u_i[NQ * chunk + low // OWN : NQ * chunk + high // OWN].reshape(high - low, E)
        value = jnp.exp2(dot_nt(u_j[slot], block) * RATE)
        tiles[chunk, rows_j, low:high] = value.astype(BF16)
        total = acc[rows_j, :]
        for lane in range(0, high - low, 128):
            total = total + value[:, lane : lane + 128]
        acc[rows_j, :] = total

    def tile_range(first, last, places, low=0, high=WIDE):
        for dz, dy in places:
            for chunk in range(first, last):
                tile(chunk, j_slot(dz, dy), low, high)

    near, beside = PLACES[0:4], PLACES[5:7]

    row_over(0, 0)
    for step, flip in ((0, 1), (1, 0), (3, 0), (2, 0)):
        row_piece(0, 0, step, flip)
        col_piece(0, 0, step, flip)
    for place in PLACES[1:4]:
        on_row(*place)
        on_col(*place)
    row_here(0, 0, 1)
    row_here(0, 1, 1)
    tile_range(0, 1, near)
    row_here(1, 0, 1)
    row_here(3, 0, 1)
    tile_range(1, 2, near[0:2])
    on_row(2, 0)
    on_col(2, 0)
    for dz, dy in offsets_c:
        push(start_all.at[mine], start_all.at[mine], s_st, r_st, at_c(dz, dy))
    tile_range(1, 2, near[2:4])
    tile_range(0, 2, PLACES[4:5])
    for place in PLACES[5:7]:
        on_row(*place)
        on_col(*place)
    tile_range(0, 2, beside)
    row_here(2, 0, 1)
    row_here(1, 1, 1)
    tile_range(2, 3, PLACES[0:7])
    row_here(3, 1, 1)
    tile_range(3, 4, PLACES[0:7], 0, PAIR)
    on_row(2, 1)
    on_col(2, 1)
    tile_range(0, 3, PLACES[7:8])
    tile_range(3, 4, PLACES[7:8], 0, PAIR)
    row_here(2, 1, 1)
    tile_range(3, 4, PLACES, PAIR, WIDE)
    arrived(start_all.at[0:7], r_st)

    ones = jnp.ones((8, 128), BF16)
    for slot in range(NZ):
        left = acc[slot * OWN : (slot + 1) * OWN, :]
        total = jnp.zeros((8, OWN), F32)
        for _ in range(3):
            top = left.astype(BF16)
            left = left - top.astype(F32)
            total = total + dot_nt(ones, top)
        part[0, slot : slot + 1, 0:OWN] = total[0:1, :]
    for n, (dz, dy) in enumerate(offsets_c):
        push(part.at[0], part.at[n + 1], s_pt, r_pt, at_c(dz, dy))
    arrived(part.at[1:8], r_pt)
    degrees = part[0, :, 0:OWN]
    for n in range(1, NZ):
        degrees = degrees + part[n, :, 0:OWN]
    scales = 1.0 / jnp.sqrt(degrees)
    scale_all[0] = scales
    scale_all[1] = degrees * math.exp(-8.0)
    deg_ref[...] = scale_all[1, pl.ds(mine, 1), :]
    scale = scale_all[0, pl.ds(mine, 1), :]
    for slot in range(NZ):
        lhs[:, slot * OWN : (slot + 1) * OWN] = (start_all[slot, :, 0:OWN] * scales[slot : slot + 1, :]).astype(BF16)

    def to_sibling(step, chunk, out):
        pair = pl.ds(2 * chunk, 2)
        for sub in range(2):
            sum_send[step, 2 * chunk + sub, :, 0:OWN] = out[:, sub * PAIR : sub * PAIR + OWN]
            sib_send[step, 2 * chunk + sub, :, 0:OWN] = out[:, sub * PAIR + OWN : (sub + 1) * PAIR]
        push(sib_send.at[step, pair], sib_recv.at[step, pair], s_sb.at[step], r_sb.at[step, chunk], sibling)

    def to_owners(step, chunk):
        arrived(sib_recv.at[step, pl.ds(2 * chunk, 2)], r_sb.at[step, chunk])
        for n in (2 * chunk + 1, 2 * chunk):
            dx, dy = PLACES[n]
            sum_send[step, n, :, 0:OWN] += sib_recv[step, n, :, 0:OWN]
            if n:
                push(sum_send.at[step, n], sum_recv.at[step, n], s_sm.at[step], r_sm.at[step], at_r(-dx, dy))

    def gathered(step):
        arrived(sum_recv.at[step, 1:8], r_sm.at[step])
        total = sum_send[step, 0, :, 0:OWN]
        for n in range(1, NZ):
            total = total + sum_recv[step, n, :, 0:OWN]
        return total * scale

    for chunk in (3, 2, 1, 0):
        to_sibling(0, chunk, jnp.dot(lhs[...], tiles[chunk], preferred_element_type=F32))
        if chunk < 3:
            to_owners(0, chunk + 1)
    to_owners(0, 0)
    image = gathered(0)

    raw = image * scale
    high = raw.astype(BF16)
    raw_all[mine, 0:K, 0:OWN] = high
    raw_all[mine, K : 2 * K, 0:OWN] = (raw - high.astype(F32)).astype(BF16)
    for dz, dy in ((0, 1), (1, 1), (3, 1), (2, 1), (2, 0), (1, 0), (3, 0)):
        push(raw_all.at[mine], raw_all.at[mine], s_rw, r_rw.at[dz, dy], at_c(dz, dy))

    def gram_start(step, image):
        gram_c[step, 0] = pack(dot_nt(image, image, HIGH))
        for n, (dz, dy) in enumerate(offsets_c):
            push(gram_c.at[step, 0], gram_c.at[step, n + 1], s_gc.at[step], r_gc.at[step], at_c(dz, dy))

    def gram_middle(step):
        arrived(gram_c.at[step, 1:8], r_gc.at[step])
        gram = gram_c[step, 0]
        for n in range(1, NZ):
            gram = gram + gram_c[step, n]
        gram_r[step, 0] = gram
        for n, (dx, dy, dc) in enumerate(offsets_r):
            push(gram_r.at[step, 0], gram_r.at[step, n + 1], s_gr.at[step], r_gr.at[step], at_r(dx, dy, dc))

    def gram_end(step):
        arrived(gram_r.at[step, 1:16], r_gr.at[step])
        gram = gram_r[step, 0]
        for n in range(1, 2 * NZ):
            gram = gram + gram_r[step, n]
        return inverse_factor(unpack(gram))

    gram_start(0, image)

    def product(dz, chunk):
        rows = pl.ds(pl.multiple_of(lax.rem(z - dz + NQ, NQ) * PAIR, PAIR), PAIR)
        out = jnp.dot(lhs_pair[dz], tiles[chunk, rows, :], preferred_element_type=F32)
        return out[0:K] + out[K : 2 * K]

    def ready(dz):
        first = lax.rem(z - dz + NQ, NQ) * 2
        for dy in range(2):
            if dz or dy:
                arrived(raw_all.at[j_slot(dz, dy)], r_rw.at[dz, dy])
        lhs_pair[dz, :, 0:OWN] = raw_all[first, :, 0:OWN]
        lhs_pair[dz, :, OWN:PAIR] = raw_all[first + 1, :, 0:OWN]

    ready(0)
    for chunk in range(4):
        out_acc[chunk] = product(0, chunk)
    ready(1)
    ready(3)
    for chunk in (3, 2):
        out_acc[chunk] += product(1, chunk) + product(3, chunk)
    gram_middle(0)
    ready(2)
    for chunk in (3, 2):
        to_sibling(1, chunk, out_acc[chunk] + product(2, chunk))
    to_owners(1, 3)
    for chunk in (1, 0):
        to_sibling(1, chunk, out_acc[chunk] + product(1, chunk) + product(3, chunk) + product(2, chunk))
        to_owners(1, chunk + 1)
    to_owners(1, 0)
    inverse = gram_end(0)
    image = gathered(1)
    image = jnp.dot(inverse, image, precision=HIGH, preferred_element_type=F32)
    gram_start(1, image)
    gram_middle(1)
    inverse = gram_end(1)
    vec_ref[...] = jnp.dot(inverse, image, precision=HIGH, preferred_element_type=F32)

    sent(u_i.at[0:15], s_i)
    sent(u_j.at[0:7], s_j)
    sent(start_all.at[0:7], s_st)
    sent(part.at[1:8], s_pt)
    sent(raw_all.at[0:7], s_rw)
    for step in range(2):
        sent(sib_send.at[step], s_sb.at[step])
        sent(sum_send.at[step, 1:8], s_sm.at[step])
        sent(gram_c.at[step, 1:8], s_gc.at[step])
        sent(gram_r.at[step, 1:16], s_gr.at[step])


def local(embeddings, start_vectors):
    dma = pltpu.SemaphoreType.DMA
    vmem = pltpu.VMEM
    vectors, degrees = pl.pallas_call(
        kernel,
        out_shape=(vmem((K, OWN), F32), vmem((1, OWN), F32)),
        in_specs=[pl.BlockSpec(memory_space=vmem)] * 2,
        out_specs=(pl.BlockSpec(memory_space=vmem), pl.BlockSpec(memory_space=vmem)),
        scratch_shapes=[
            vmem((NQ * NQ, OWN, E), BF16),
            vmem((NZ, OWN, E), BF16),
            vmem((NQ, J, WIDE), BF16),
            vmem((J, 128), F32),
            vmem((NZ, K, PAD), F32),
            vmem((NZ, NZ, PAD), F32),
            vmem((2, NZ, OWN), F32),
            vmem((K, J), BF16),
            vmem((NQ, 2 * K, PAIR), BF16),
            vmem((NQ, K, WIDE), F32),
            vmem((2, NZ, K, PAD), F32),
            vmem((2, NZ, K, PAD), F32),
            vmem((2, NZ, K, PAD), F32),
            vmem((2, NZ, K, PAD), F32),
            vmem((NZ, 2 * K, PAD), BF16),
            vmem((2, NZ, 8, 128), F32),
            vmem((2, 2 * NZ, 8, 128), F32),
            dma, dma((2 * NZ,)),
            dma, dma((NQ, 2)),
            dma, dma,
            dma, dma,
            dma((2,)), dma((2, NQ)),
            dma((2,)), dma((2,)),
            dma, dma((NQ, 2)),
            dma((2,)), dma((2,)),
            dma((2,)), dma((2,)),
        ],
        compiler_params=pltpu.CompilerParams(
            collective_id=0, has_side_effects=True, vmem_limit_bytes=56 * 2**20
        ),
        name="subspace",
    )(embeddings, start_vectors)
    return (vectors, degrees.reshape(OWN))


def solution(mesh):
    return jax.shard_map(
        local,
        mesh=mesh,
        in_specs=(P(("row", "col"), None), P(None, ("row", "col"))),
        out_specs=(P(None, ("row", "col")), P(("row", "col"))),
        check_vma=False,
    )
```

```python
import math

import jax
import jax.numpy as jnp
from jax import lax
from jax.experimental import pallas as pl
from jax.experimental.pallas import tpu as pltpu
from jax.sharding import PartitionSpec as P

K = 32
PLACES = ((0, 0), (0, 1), (1, 0), (3, 0), (2, 0), (1, 1), (3, 1), (2, 1))
E = 256
OWN = 320
PAD = 384
NZ = 8
NQ = 4
J = NZ * OWN
PAIR = 2 * OWN
WIDE = NQ * OWN
RATE = 8.0 / math.log(2.0)
MESH = pl.DeviceIdType.MESH
HIGH = lax.Precision.HIGHEST
F32 = jnp.float32
BF16 = jnp.bfloat16


def dot_nt(a, b, precision=None):
    return lax.dot_general(a, b, (((1,), (1,)), ((), ())), precision=precision, preferred_element_type=F32)


def pack(square):
    return jnp.concatenate([square[8 * b : 8 * b + 8, :] for b in range(4)], axis=1)


def unpack(packed):
    return jnp.concatenate([packed[:, K * b : K * b + K] for b in range(4)], axis=0)


def inverse_factor(gram):
    shape = (8, 2 * K)
    ranks = lax.broadcasted_iota(jnp.int32, (8, K), 0)
    lanes = lax.broadcasted_iota(jnp.int32, (8, K), 1)
    rank = lax.broadcasted_iota(jnp.int32, shape, 0)
    work = [
        jnp.concatenate([gram[8 * b : 8 * b + 8], (lanes == ranks + 8 * b).astype(F32)], axis=1) for b in range(4)
    ]
    done = []
    for b in range(4):
        rows = [jnp.broadcast_to(work[b][i : i + 1], shape) for i in range(8)]
        columns = [
            [jnp.broadcast_to(work[c][:, 8 * b + i : 8 * b + i + 1], shape) for c in range(b, 4)] for i in range(8)
        ]
        corner = [[jnp.broadcast_to(columns[j][0][i : i + 1], shape) for j in range(i + 1)] for i in range(8)]
        pivots = corner[0][0]
        for i in range(8):
            pivots = jnp.where(rank == i, corner[i][i], pivots)
            inverse = 1.0 / corner[i][i]
            factors = [column * inverse for column in columns[i]]
            factors[0] = jnp.where(rank > i, factors[0], 0.0)
            for j in range(i + 1, 8):
                factor = corner[j][i] * inverse
                rows[j] = rows[j] - factor * rows[i]
                columns[j] = [old - own * corner[j][i] for old, own in zip(columns[j], factors)]
                for k in range(i + 1, j + 1):
                    corner[j][k] = corner[j][k] - factor * corner[k][i]
            for c in range(b, 4):
                work[c] = work[c] - factors[c - b] * rows[i]
        done.append(work[b] * (1.0 / jnp.sqrt(pivots)))
    return jnp.concatenate(done, axis=0)[:, K : 2 * K]


def kernel(
    emb_ref, start_ref, vec_ref, deg_ref,
    u_i, u_j, tiles, acc, start_all, part, scale_all, lhs, lhs_pair, out_acc,
    send, recv, own_ref, sib_send, sib_recv, sum_send, sum_recv, raw_all, gram_c, gram_r,
    s_i, r_i, s_j, r_j, s_st, r_st, s_pt, r_pt, s_1, r_1, s_sb, r_sb, s_sm, r_sm, s_rw, r_rw, s_gc, r_gc, s_gr, r_gr,
):
    row = lax.axis_index("row")
    col = lax.axis_index("col")
    z, core = row // 2, row % 2
    x, y = col % NQ, col // NQ
    y_rows = y + 1 - 2 * (y % 2)
    y_cols = NQ - 1 - y
    sibling = (z * 2 + 1 - core, col)

    def at_r(dx, dy, dc=0):
        place = (y_rows if dy else y) * NQ + lax.rem(x + dx + NQ, NQ)
        return (z * 2 + (1 - core if dc else core), place)

    def at_c(dz, dy):
        return (lax.rem(z + dz + NQ, NQ) * 2 + core, (y_cols if dy else y) * NQ + x)

    def j_slot(dz, dy):
        return lax.rem(z - dz + NQ, NQ) * 2 + (y // 2) + dy * (1 - 2 * (y // 2))

    offsets_c = [(dz, dy) for dz, dy in PLACES if dz or dy]
    offsets_r = [(dx, dy, dc) for dx, dy in PLACES for dc in range(2) if dx or dy or dc]
    mine = j_slot(0, 0)

    def push(src, dst, s_sem, r_sem, device):
        pltpu.make_async_remote_copy(
            src_ref=src, dst_ref=dst, send_sem=s_sem, recv_sem=r_sem, device_id=device, device_id_type=MESH
        ).start()

    def arrived(ref, r_sem):
        pltpu.make_async_remote_copy(
            src_ref=ref, dst_ref=ref, send_sem=r_sem, recv_sem=r_sem, device_id=sibling, device_id_type=MESH
        ).wait_recv()

    def sent(ref, s_sem):
        pltpu.make_async_remote_copy(
            src_ref=ref, dst_ref=ref, send_sem=s_sem, recv_sem=s_sem, device_id=sibling, device_id_type=MESH
        ).wait_send()

    barrier = pltpu.get_barrier_semaphore()
    neighbours = [at(*place) for at in (at_r, at_c) for place in PLACES[1:5]] + [sibling]
    for device in neighbours:
        pl.semaphore_signal(barrier, inc=1, device_id=device, device_id_type=MESH)

    values = emb_ref[...].astype(F32)
    power = jnp.mean(values * values, axis=1, keepdims=True)
    unit = (values * lax.rsqrt(power + 1e-06) * (1.0 / math.sqrt(E))).astype(BF16)
    u_i[0] = unit
    u_j[mine] = unit
    start_all[mine, :, 0:OWN] = start_ref[...].astype(BF16)
    acc[...] = jnp.zeros_like(acc)
    pl.semaphore_wait(barrier, len(neighbours))

    def i_slot(dx, dy, dc=0):
        return 2 * PLACES.index((dx % NQ, dy)) + dc

    def row_piece(dx, dy, step, flip):
        to = i_slot(dx + step, dy ^ flip)
        push(u_i.at[i_slot(dx, dy)], u_i.at[to], s_i, r_i.at[to], at_r(step, flip))

    def row_over(dx, dy):
        push(u_i.at[i_slot(dx, dy)], u_i.at[i_slot(dx, dy, 1)], s_i, r_i.at[i_slot(dx, dy, 1)], sibling)

    def row_here(dx, dy, dc=0):
        arrived(u_i.at[i_slot(dx, dy, dc)], r_i.at[i_slot(dx, dy, dc)])

    def col_piece(dz, dy, step, flip):
        slot = j_slot(dz, dy)
        push(u_j.at[slot], u_j.at[slot], s_j, r_j.at[(dz + step) % NQ, dy ^ flip], at_c(step, flip))

    def col_here(dz, dy):
        arrived(u_j.at[j_slot(dz, dy)], r_j.at[dz, dy])

    def onward(piece, d, dy):
        if (d, dy) == (0, 1):

            @pl.when(core == 0)
            def _():
                for step in (1, 3, 2):
                    piece(0, 1, step, 0)

        elif dy == 0:
            pl.when(core == 1)(lambda: piece(d, 0, 0, 1))

    def on_row(dx, dy):
        row_here(dx, dy)
        onward(row_piece, dx, dy)
        row_over(dx, dy)

    def on_col(dz, dy):
        col_here(dz, dy)
        onward(col_piece, dz, dy)

    def tile(chunk, slot, low=0, high=WIDE):
        rows_j = pl.ds(pl.multiple_of(slot * OWN, OWN), OWN)
        block = u_i[NQ * chunk + low // OWN : NQ * chunk + high // OWN].reshape(high - low, E)
        value = jnp.exp2(dot_nt(u_j[slot], block) * RATE)
        tiles[chunk, rows_j, low:high] = value.astype(BF16)
        total = acc[rows_j, :]
        for lane in range(0, high - low, 128):
            total = total + value[:, lane : lane + 128]
        acc[rows_j, :] = total

    def tile_range(first, last, places, low=0, high=WIDE):
        for dz, dy in places:
            for chunk in range(first, last):
                tile(chunk, j_slot(dz, dy), low, high)

    near, beside = PLACES[0:4], PLACES[5:7]

    row_over(0, 0)
    for step, flip in ((0, 1), (1, 0), (3, 0), (2, 0)):
        row_piece(0, 0, step, flip)
        col_piece(0, 0, step, flip)
    for place in PLACES[1:4]:
        on_row(*place)
        on_col(*place)
    row_here(0, 0, 1)
    row_here(0, 1, 1)
    tile_range(0, 1, near)
    row_here(1, 0, 1)
    row_here(3, 0, 1)
    tile_range(1, 2, near[0:2])
    on_row(2, 0)
    on_col(2, 0)
    tile_range(1, 2, near[2:4])
    tile_range(0, 2, PLACES[4:5])
    for place in PLACES[5:7]:
        on_row(*place)
        on_col(*place)
    tile_range(0, 2, beside)
    row_here(2, 0, 1)
    row_here(1, 1, 1)
    tile_range(2, 3, PLACES[0:7])
    row_here(3, 1, 1)
    tile_range(3, 4, PLACES[0:7], 0, PAIR)
    on_row(2, 1)
    on_col(2, 1)
    for dz, dy in offsets_c:
        push(start_all.at[mine], start_all.at[mine], s_st, r_st, at_c(dz, dy))
    tile_range(0, 3, PLACES[7:8])
    tile_range(3, 4, PLACES[7:8], 0, PAIR)
    row_here(2, 1, 1)
    tile_range(3, 4, PLACES, PAIR, WIDE)

    ones = jnp.ones((8, 128), BF16)
    for slot in range(NZ):
        left = acc[slot * OWN : (slot + 1) * OWN, :]
        total = jnp.zeros((8, OWN), F32)
        for _ in range(3):
            top = left.astype(BF16)
            left = left - top.astype(F32)
            total = total + dot_nt(ones, top)
        part[0, slot : slot + 1, 0:OWN] = total[0:1, :]
    for n, (dz, dy) in enumerate(offsets_c):
        push(part.at[0], part.at[n + 1], s_pt, r_pt, at_c(dz, dy))
    arrived(part.at[1:8], r_pt)
    degrees = part[0, :, 0:OWN]
    for n in range(1, NZ):
        degrees = degrees + part[n, :, 0:OWN]
    scales = 1.0 / jnp.sqrt(degrees)
    scale_all[0] = scales
    scale_all[1] = degrees * math.exp(-8.0)
    deg_ref[...] = scale_all[1, pl.ds(mine, 1), :]
    scale = scale_all[0, pl.ds(mine, 1), :]
    arrived(start_all.at[0:7], r_st)
    for slot in range(NZ):
        lhs[:, slot * OWN : (slot + 1) * OWN] = (start_all[slot, :, 0:OWN].astype(F32) * scales[slot : slot + 1, :]).astype(BF16)

    for chunk in (3, 2, 1, 0):
        out = jnp.dot(lhs[...], tiles[chunk], preferred_element_type=F32)
        for sub in range(NQ):
            slot = NQ * chunk + sub
            block = out[:, sub * OWN : (sub + 1) * OWN]
            if slot == 0:
                own_ref[...] = block
            else:
                dx, dy = PLACES[slot // 2]
                send[slot, :, 0:OWN] = block.astype(BF16)
                push(send.at[slot], recv.at[slot], s_1, r_1, at_r(-dx, dy, slot % 2))
    arrived(recv.at[1:16], r_1)
    image = own_ref[...]
    for slot in range(1, 2 * NZ):
        image = image + recv[slot, :, 0:OWN].astype(F32)
    image = image * scale

    raw = image * scale
    high = raw.astype(BF16)
    raw_all[mine, 0:K, 0:OWN] = high
    raw_all[mine, K : 2 * K, 0:OWN] = (raw - high.astype(F32)).astype(BF16)
    for dz, dy in ((0, 1), (1, 1), (3, 1), (2, 1), (2, 0), (1, 0), (3, 0)):
        push(raw_all.at[mine], raw_all.at[mine], s_rw, r_rw.at[dz, dy], at_c(dz, dy))

    def gram_start(step, image):
        gram_c[step, 0] = pack(dot_nt(image, image, HIGH))
        for n, (dz, dy) in enumerate(offsets_c):
            push(gram_c.at[step, 0], gram_c.at[step, n + 1], s_gc.at[step], r_gc.at[step], at_c(dz, dy))

    def gram_middle(step):
        arrived(gram_c.at[step, 1:8], r_gc.at[step])
        gram = gram_c[step, 0]
        for n in range(1, NZ):
            gram = gram + gram_c[step, n]
        gram_r[step, 0] = gram
        for n, (dx, dy, dc) in enumerate(offsets_r):
            push(gram_r.at[step, 0], gram_r.at[step, n + 1], s_gr.at[step], r_gr.at[step], at_r(dx, dy, dc))

    def gram_end(step):
        arrived(gram_r.at[step, 1:16], r_gr.at[step])
        gram = gram_r[step, 0]
        for n in range(1, 2 * NZ):
            gram = gram + gram_r[step, n]
        return inverse_factor(unpack(gram))

    gram_start(0, image)

    def to_sibling(chunk, out):
        pair = pl.ds(2 * chunk, 2)
        for sub in range(2):
            sum_send[2 * chunk + sub, :, 0:OWN] = out[:, sub * PAIR : sub * PAIR + OWN]
            sib_send[2 * chunk + sub, :, 0:OWN] = out[:, sub * PAIR + OWN : (sub + 1) * PAIR]
        push(sib_send.at[pair], sib_recv.at[pair], s_sb, r_sb.at[chunk], sibling)

    def to_owners(chunk):
        arrived(sib_recv.at[pl.ds(2 * chunk, 2)], r_sb.at[chunk])
        for n in (2 * chunk + 1, 2 * chunk):
            dx, dy = PLACES[n]
            sum_send[n, :, 0:OWN] += sib_recv[n, :, 0:OWN]
            if n:
                push(sum_send.at[n], sum_recv.at[n], s_sm, r_sm, at_r(-dx, dy))

    def product(dz, chunk):
        rows = pl.ds(pl.multiple_of(lax.rem(z - dz + NQ, NQ) * PAIR, PAIR), PAIR)
        out = jnp.dot(lhs_pair[dz], tiles[chunk, rows, :], preferred_element_type=F32)
        return out[0:K] + out[K : 2 * K]

    def ready(dz):
        first = lax.rem(z - dz + NQ, NQ) * 2
        for dy in range(2):
            if dz or dy:
                arrived(raw_all.at[j_slot(dz, dy)], r_rw.at[dz, dy])
        lhs_pair[dz, :, 0:OWN] = raw_all[first, :, 0:OWN]
        lhs_pair[dz, :, OWN:PAIR] = raw_all[first + 1, :, 0:OWN]

    ready(0)
    for chunk in range(4):
        out_acc[chunk] = product(0, chunk)
    ready(1)
    ready(3)
    for chunk in range(4):
        out_acc[chunk] += product(1, chunk) + product(3, chunk)
    gram_middle(0)
    ready(2)
    for chunk in (3, 2, 1, 0):
        to_sibling(chunk, out_acc[chunk] + product(2, chunk))
        if chunk < 3:
            to_owners(chunk + 1)
    to_owners(0)
    inverse = gram_end(0)
    arrived(sum_recv.at[1:8], r_sm)
    image = sum_send[0, :, 0:OWN]
    for n in range(1, NZ):
        image = image + sum_recv[n, :, 0:OWN]
    image = image * scale
    image = jnp.dot(inverse, image, precision=HIGH, preferred_element_type=F32)
    gram_start(1, image)
    gram_middle(1)
    inverse = gram_end(1)
    vec_ref[...] = jnp.dot(inverse, image, precision=HIGH, preferred_element_type=F32)

    sent(u_i.at[0:15], s_i)
    sent(u_j.at[0:7], s_j)
    sent(start_all.at[0:7], s_st)
    sent(part.at[1:8], s_pt)
    sent(raw_all.at[0:7], s_rw)
    sent(send.at[1:16], s_1)
    sent(sib_send, s_sb)
    sent(sum_send.at[1:8], s_sm)
    for step in range(2):
        sent(gram_c.at[step, 1:8], s_gc.at[step])
        sent(gram_r.at[step, 1:16], s_gr.at[step])


def local(embeddings, start_vectors):
    dma = pltpu.SemaphoreType.DMA
    vmem = pltpu.VMEM
    vectors, degrees = pl.pallas_call(
        kernel,
        out_shape=(vmem((K, OWN), F32), vmem((1, OWN), F32)),
        in_specs=[pl.BlockSpec(memory_space=vmem)] * 2,
        out_specs=(pl.BlockSpec(memory_space=vmem), pl.BlockSpec(memory_space=vmem)),
        scratch_shapes=[
            vmem((NQ * NQ, OWN, E), BF16),
            vmem((NZ, OWN, E), BF16),
            vmem((NQ, J, WIDE), BF16),
            vmem((J, 128), F32),
            vmem((NZ, K, PAD), BF16),
            vmem((NZ, NZ, PAD), F32),
            vmem((2, NZ, OWN), F32),
            vmem((K, J), BF16),
            vmem((NQ, 2 * K, PAIR), BF16),
            vmem((NQ, K, WIDE), F32),
            vmem((2 * NZ, K, PAD), BF16),
            vmem((2 * NZ, K, PAD), BF16),
            vmem((K, OWN), F32),
            vmem((NZ, K, PAD), F32),
            vmem((NZ, K, PAD), F32),
            vmem((NZ, K, PAD), F32),
            vmem((NZ, K, PAD), F32),
            vmem((NZ, 2 * K, PAD), BF16),
            vmem((2, NZ, 8, 128), F32),
            vmem((2, 2 * NZ, 8, 128), F32),
            dma, dma((2 * NZ,)),
            dma, dma((NQ, 2)),
            dma, dma,
            dma, dma,
            dma, dma,
            dma, dma((NQ,)),
            dma, dma,
            dma, dma((NQ, 2)),
            dma((2,)), dma((2,)),
            dma((2,)), dma((2,)),
        ],
        compiler_params=pltpu.CompilerParams(
            collective_id=0, has_side_effects=True, vmem_limit_bytes=56 * 2**20
        ),
        name="subspace",
    )(embeddings, start_vectors)
    return (vectors, degrees.reshape(OWN))


def solution(mesh):
    return jax.shard_map(
        local,
        mesh=mesh,
        in_specs=(P(("row", "col"), None), P(None, ("row", "col"))),
        out_specs=(P(None, ("row", "col")), P(("row", "col"))),
        check_vma=False,
    )
```

```python
import math

import jax
import jax.numpy as jnp
from jax import lax
from jax.experimental import pallas as pl
from jax.experimental.pallas import tpu as pltpu
from jax.sharding import PartitionSpec as P

K = 32
PLACES = ((0, 0), (0, 1), (1, 0), (3, 0), (2, 0), (1, 1), (3, 1), (2, 1))
E = 256
OWN = 320
PAD = 384
NZ = 8
NQ = 4
J = NZ * OWN
PAIR = 2 * OWN
WIDE = NQ * OWN
RATE = 8.0 / math.log(2.0)
MESH = pl.DeviceIdType.MESH
HIGH = lax.Precision.HIGHEST
F32 = jnp.float32
BF16 = jnp.bfloat16


def dot_nt(a, b, precision=None):
    return lax.dot_general(a, b, (((1,), (1,)), ((), ())), precision=precision, preferred_element_type=F32)


def pack(square):
    return jnp.concatenate([square[8 * b : 8 * b + 8, :] for b in range(4)], axis=1)


def unpack(packed):
    return jnp.concatenate([packed[:, K * b : K * b + K] for b in range(4)], axis=0)


def fold(wide):
    n = wide.shape[0]
    rest = [wide[n // 4 * b : n // 4 * (b + 1), 256:OWN] for b in range(4)]
    return jnp.concatenate([wide[:, 0:256], jnp.concatenate(rest, axis=1)], axis=0)


def unfold(folded):
    n = folded.shape[0] // 5 * 4
    rest = [folded[n:, 64 * b : 64 * (b + 1)] for b in range(4)]
    return jnp.concatenate([folded[0:n], jnp.concatenate(rest, axis=0)], axis=1)


def inverse_factor(gram):
    shape = (8, 2 * K)
    ranks = lax.broadcasted_iota(jnp.int32, (8, K), 0)
    lanes = lax.broadcasted_iota(jnp.int32, (8, K), 1)
    rank = lax.broadcasted_iota(jnp.int32, shape, 0)
    work = [
        jnp.concatenate([gram[8 * b : 8 * b + 8], (lanes == ranks + 8 * b).astype(F32)], axis=1) for b in range(4)
    ]
    done = []
    for b in range(4):
        rows = [jnp.broadcast_to(work[b][i : i + 1], shape) for i in range(8)]
        columns = [
            [jnp.broadcast_to(work[c][:, 8 * b + i : 8 * b + i + 1], shape) for c in range(b, 4)] for i in range(8)
        ]
        corner = [[jnp.broadcast_to(columns[j][0][i : i + 1], shape) for j in range(i + 1)] for i in range(8)]
        pivots = corner[0][0]
        for i in range(8):
            pivots = jnp.where(rank == i, corner[i][i], pivots)
            inverse = 1.0 / corner[i][i]
            factors = [column * inverse for column in columns[i]]
            factors[0] = jnp.where(rank > i, factors[0], 0.0)
            for j in range(i + 1, 8):
                factor = corner[j][i] * inverse
                rows[j] = rows[j] - factor * rows[i]
                columns[j] = [old - own * corner[j][i] for old, own in zip(columns[j], factors)]
                for k in range(i + 1, j + 1):
                    corner[j][k] = corner[j][k] - factor * corner[k][i]
            for c in range(b, 4):
                work[c] = work[c] - factors[c - b] * rows[i]
        done.append(work[b] * (1.0 / jnp.sqrt(pivots)))
    return jnp.concatenate(done, axis=0)[:, K : 2 * K]


def kernel(
    emb_ref, start_ref, vec_ref, deg_ref,
    u_i, u_j, tiles, acc, start_all, part, scale_all, lhs, lhs_pair, out_acc,
    send, recv, own_ref, sib_send, sib_recv, sum_send, sum_recv, raw_all, gram_c, gram_r,
    s_i, r_i, s_j, r_j, s_st, r_st, s_pt, r_pt, s_1, r_1, s_sb, r_sb, s_sm, r_sm, s_rw, r_rw, s_gc, r_gc, s_gr, r_gr,
):
    row = lax.axis_index("row")
    col = lax.axis_index("col")
    z, core = row // 2, row % 2
    x, y = col % NQ, col // NQ
    y_rows = y + 1 - 2 * (y % 2)
    y_cols = NQ - 1 - y
    sibling = (z * 2 + 1 - core, col)

    def at_r(dx, dy, dc=0):
        place = (y_rows if dy else y) * NQ + lax.rem(x + dx + NQ, NQ)
        return (z * 2 + (1 - core if dc else core), place)

    def at_c(dz, dy):
        return (lax.rem(z + dz + NQ, NQ) * 2 + core, (y_cols if dy else y) * NQ + x)

    def j_slot(dz, dy):
        return lax.rem(z - dz + NQ, NQ) * 2 + (y // 2) + dy * (1 - 2 * (y // 2))

    offsets_c = [(dz, dy) for dz, dy in PLACES if dz or dy]
    offsets_r = [(dx, dy, dc) for dx, dy in PLACES for dc in range(2) if dx or dy or dc]
    mine = j_slot(0, 0)

    def push(src, dst, s_sem, r_sem, device):
        pltpu.make_async_remote_copy(
            src_ref=src, dst_ref=dst, send_sem=s_sem, recv_sem=r_sem, device_id=device, device_id_type=MESH
        ).start()

    def arrived(ref, r_sem):
        pltpu.make_async_remote_copy(
            src_ref=ref, dst_ref=ref, send_sem=r_sem, recv_sem=r_sem, device_id=sibling, device_id_type=MESH
        ).wait_recv()

    def sent(ref, s_sem):
        pltpu.make_async_remote_copy(
            src_ref=ref, dst_ref=ref, send_sem=s_sem, recv_sem=s_sem, device_id=sibling, device_id_type=MESH
        ).wait_send()

    barrier = pltpu.get_barrier_semaphore()
    neighbours = [at(*place) for at in (at_r, at_c) for place in PLACES[1:5]] + [sibling]
    for device in neighbours:
        pl.semaphore_signal(barrier, inc=1, device_id=device, device_id_type=MESH)

    values = emb_ref[...].astype(F32)
    power = jnp.mean(values * values, axis=1, keepdims=True)
    unit = (values * lax.rsqrt(power + 1e-06) * (1.0 / math.sqrt(E))).astype(BF16)
    u_i[0] = unit
    u_j[mine] = unit
    start_all[mine, :, 0:OWN] = start_ref[...].astype(BF16)
    acc[...] = jnp.zeros_like(acc)
    pl.semaphore_wait(barrier, len(neighbours))

    def i_slot(dx, dy, dc=0):
        return 2 * PLACES.index((dx % NQ, dy)) + dc

    def row_piece(dx, dy, step, flip):
        to = i_slot(dx + step, dy ^ flip)
        push(u_i.at[i_slot(dx, dy)], u_i.at[to], s_i, r_i.at[to], at_r(step, flip))

    def row_over(dx, dy):
        push(u_i.at[i_slot(dx, dy)], u_i.at[i_slot(dx, dy, 1)], s_i, r_i.at[i_slot(dx, dy, 1)], sibling)

    def row_here(dx, dy, dc=0):
        arrived(u_i.at[i_slot(dx, dy, dc)], r_i.at[i_slot(dx, dy, dc)])

    def col_piece(dz, dy, step, flip):
        slot = j_slot(dz, dy)
        push(u_j.at[slot], u_j.at[slot], s_j, r_j.at[(dz + step) % NQ, dy ^ flip], at_c(step, flip))

    def col_here(dz, dy):
        arrived(u_j.at[j_slot(dz, dy)], r_j.at[dz, dy])

    def onward(piece, d, dy):
        if (d, dy) == (0, 1):

            @pl.when(core == 0)
            def _():
                for step in (1, 3, 2):
                    piece(0, 1, step, 0)

        elif dy == 0:
            pl.when(core == 1)(lambda: piece(d, 0, 0, 1))

    def on_row(dx, dy):
        row_here(dx, dy)
        onward(row_piece, dx, dy)
        row_over(dx, dy)

    def on_col(dz, dy):
        col_here(dz, dy)
        onward(col_piece, dz, dy)

    def tile(chunk, slot, low=0, high=WIDE):
        rows_j = pl.ds(pl.multiple_of(slot * OWN, OWN), OWN)
        block = u_i[NQ * chunk + low // OWN : NQ * chunk + high // OWN].reshape(high - low, E)
        value = jnp.exp2(dot_nt(u_j[slot], block) * RATE)
        tiles[chunk, rows_j, low:high] = value.astype(BF16)
        total = acc[rows_j, :]
        for lane in range(0, high - low, 128):
            total = total + value[:, lane : lane + 128]
        acc[rows_j, :] = total

    def tile_range(first, last, places, low=0, high=WIDE):
        for dz, dy in places:
            for chunk in range(first, last):
                tile(chunk, j_slot(dz, dy), low, high)

    near, beside = PLACES[0:4], PLACES[5:7]

    row_over(0, 0)
    for step, flip in ((0, 1), (1, 0), (3, 0), (2, 0)):
        row_piece(0, 0, step, flip)
        col_piece(0, 0, step, flip)
    for place in PLACES[1:4]:
        on_row(*place)
        on_col(*place)
    row_here(0, 0, 1)
    row_here(0, 1, 1)
    tile_range(0, 1, near)
    row_here(1, 0, 1)
    row_here(3, 0, 1)
    tile_range(1, 2, near[0:2])
    on_row(2, 0)
    on_col(2, 0)
    tile_range(1, 2, near[2:4])
    tile_range(0, 2, PLACES[4:5])
    for place in PLACES[5:7]:
        on_row(*place)
        on_col(*place)
    tile_range(0, 2, beside)
    row_here(2, 0, 1)
    row_here(1, 1, 1)
    tile_range(2, 3, PLACES[0:7])
    row_here(3, 1, 1)
    tile_range(3, 4, PLACES[0:7], 0, PAIR)
    on_row(2, 1)
    on_col(2, 1)
    for dz, dy in offsets_c:
        push(start_all.at[mine], start_all.at[mine], s_st, r_st, at_c(dz, dy))
    tile_range(0, 3, PLACES[7:8])
    tile_range(3, 4, PLACES[7:8], 0, PAIR)
    row_here(2, 1, 1)
    tile_range(3, 4, PLACES, PAIR, WIDE)

    ones = jnp.ones((8, 128), BF16)
    for slot in range(NZ):
        left = acc[slot * OWN : (slot + 1) * OWN, :]
        total = jnp.zeros((8, OWN), F32)
        for _ in range(3):
            top = left.astype(BF16)
            left = left - top.astype(F32)
            total = total + dot_nt(ones, top)
        part[0, slot : slot + 1, 0:OWN] = total[0:1, :]
    for n, (dz, dy) in enumerate(offsets_c):
        push(part.at[0], part.at[n + 1], s_pt, r_pt, at_c(dz, dy))
    arrived(part.at[1:8], r_pt)
    degrees = part[0, :, 0:OWN]
    for n in range(1, NZ):
        degrees = degrees + part[n, :, 0:OWN]
    scales = 1.0 / jnp.sqrt(degrees)
    scale_all[0] = scales
    scale_all[1] = degrees * math.exp(-8.0)
    deg_ref[...] = scale_all[1, pl.ds(mine, 1), :]
    scale = scale_all[0, pl.ds(mine, 1), :]
    arrived(start_all.at[0:7], r_st)
    for slot in range(NZ):
        lhs[:, slot * OWN : (slot + 1) * OWN] = (start_all[slot, :, 0:OWN].astype(F32) * scales[slot : slot + 1, :]).astype(BF16)

    for chunk in (3, 2, 1, 0):
        out = jnp.dot(lhs[...], tiles[chunk], preferred_element_type=F32)
        for sub in range(NQ):
            slot = NQ * chunk + sub
            block = out[:, sub * OWN : (sub + 1) * OWN]
            if slot == 0:
                own_ref[...] = block
            else:
                dx, dy = PLACES[slot // 2]
                send[slot, :, 0:OWN] = block.astype(BF16)
                push(send.at[slot], recv.at[slot], s_1, r_1, at_r(-dx, dy, slot % 2))
    arrived(recv.at[1:16], r_1)
    image = own_ref[...]
    for slot in range(1, 2 * NZ):
        image = image + recv[slot, :, 0:OWN].astype(F32)
    image = image * scale

    raw = image * scale
    high = raw.astype(BF16)
    raw_all[mine] = fold(jnp.concatenate([high, (raw - high.astype(F32)).astype(BF16)], axis=0))
    for dz, dy in ((0, 1), (1, 1), (3, 1), (2, 1), (2, 0), (1, 0), (3, 0)):
        push(raw_all.at[mine], raw_all.at[mine], s_rw, r_rw.at[dz, dy], at_c(dz, dy))

    def gram_start(step, image):
        gram_c[step, 0] = pack(dot_nt(image, image, HIGH))
        for n, (dz, dy) in enumerate(offsets_c):
            push(gram_c.at[step, 0], gram_c.at[step, n + 1], s_gc.at[step], r_gc.at[step], at_c(dz, dy))

    def gram_middle(step):
        arrived(gram_c.at[step, 1:8], r_gc.at[step])
        gram = gram_c[step, 0]
        for n in range(1, NZ):
            gram = gram + gram_c[step, n]
        gram_r[step, 0] = gram
        for n, (dx, dy, dc) in enumerate(offsets_r):
            push(gram_r.at[step, 0], gram_r.at[step, n + 1], s_gr.at[step], r_gr.at[step], at_r(dx, dy, dc))

    def gram_end(step):
        arrived(gram_r.at[step, 1:16], r_gr.at[step])
        gram = gram_r[step, 0]
        for n in range(1, 2 * NZ):
            gram = gram + gram_r[step, n]
        return inverse_factor(unpack(gram))

    gram_start(0, image)

    def to_sibling(chunk, out):
        pair = pl.ds(2 * chunk, 2)
        for sub in range(2):
            sum_send[2 * chunk + sub] = fold(out[:, sub * PAIR : sub * PAIR + OWN])
            sib_send[2 * chunk + sub] = fold(out[:, sub * PAIR + OWN : (sub + 1) * PAIR])
        push(sib_send.at[pair], sib_recv.at[pair], s_sb, r_sb.at[chunk], sibling)

    def to_owners(chunk):
        arrived(sib_recv.at[pl.ds(2 * chunk, 2)], r_sb.at[chunk])
        for n in (2 * chunk + 1, 2 * chunk):
            dx, dy = PLACES[n]
            sum_send[n] += sib_recv[n]
            if n:
                push(sum_send.at[n], sum_recv.at[n], s_sm, r_sm, at_r(-dx, dy))

    def product(dz, chunk):
        rows = pl.ds(pl.multiple_of(lax.rem(z - dz + NQ, NQ) * PAIR, PAIR), PAIR)
        out = jnp.dot(lhs_pair[dz], tiles[chunk, rows, :], preferred_element_type=F32)
        return out[0:K] + out[K : 2 * K]

    def ready(dz):
        first = lax.rem(z - dz + NQ, NQ) * 2
        for dy in range(2):
            if dz or dy:
                arrived(raw_all.at[j_slot(dz, dy)], r_rw.at[dz, dy])
        lhs_pair[dz, :, 0:OWN] = unfold(raw_all[first])
        lhs_pair[dz, :, OWN:PAIR] = unfold(raw_all[first + 1])

    ready(0)
    for chunk in range(4):
        out_acc[chunk] = product(0, chunk)
    ready(1)
    ready(3)
    for chunk in range(4):
        out_acc[chunk] += product(1, chunk) + product(3, chunk)
    gram_middle(0)
    ready(2)
    for chunk in (3, 2, 1, 0):
        to_sibling(chunk, out_acc[chunk] + product(2, chunk))
        if chunk < 3:
            to_owners(chunk + 1)
    to_owners(0)
    inverse = gram_end(0)
    arrived(sum_recv.at[1:8], r_sm)
    total = sum_send[0]
    for n in range(1, NZ):
        total = total + sum_recv[n]
    image = unfold(total) * scale
    image = jnp.dot(inverse, image, precision=HIGH, preferred_element_type=F32)
    gram_start(1, image)
    gram_middle(1)
    inverse = gram_end(1)
    vec_ref[...] = jnp.dot(inverse, image, precision=HIGH, preferred_element_type=F32)

    sent(u_i.at[0:15], s_i)
    sent(u_j.at[0:7], s_j)
    sent(start_all.at[0:7], s_st)
    sent(part.at[1:8], s_pt)
    sent(raw_all.at[0:7], s_rw)
    sent(send.at[1:16], s_1)
    sent(sib_send, s_sb)
    sent(sum_send.at[1:8], s_sm)
    for step in range(2):
        sent(gram_c.at[step, 1:8], s_gc.at[step])
        sent(gram_r.at[step, 1:16], s_gr.at[step])


def local(embeddings, start_vectors):
    dma = pltpu.SemaphoreType.DMA
    vmem = pltpu.VMEM
    vectors, degrees = pl.pallas_call(
        kernel,
        out_shape=(vmem((K, OWN), F32), vmem((1, OWN), F32)),
        in_specs=[pl.BlockSpec(memory_space=vmem)] * 2,
        out_specs=(pl.BlockSpec(memory_space=vmem), pl.BlockSpec(memory_space=vmem)),
        scratch_shapes=[
            vmem((NQ * NQ, OWN, E), BF16),
            vmem((NZ, OWN, E), BF16),
            vmem((NQ, J, WIDE), BF16),
            vmem((J, 128), F32),
            vmem((NZ, K, PAD), BF16),
            vmem((NZ, NZ, PAD), F32),
            vmem((2, NZ, OWN), F32),
            vmem((K, J), BF16),
            vmem((NQ, 2 * K, PAIR), BF16),
            vmem((NQ, K, WIDE), F32),
            vmem((2 * NZ, K, PAD), BF16),
            vmem((2 * NZ, K, PAD), BF16),
            vmem((K, OWN), F32),
            vmem((NZ, K + K // 4, 256), F32),
            vmem((NZ, K + K // 4, 256), F32),
            vmem((NZ, K + K // 4, 256), F32),
            vmem((NZ, K + K // 4, 256), F32),
            vmem((NZ, 2 * K + K // 2, 256), BF16),
            vmem((2, NZ, 8, 128), F32),
            vmem((2, 2 * NZ, 8, 128), F32),
            dma, dma((2 * NZ,)),
            dma, dma((NQ, 2)),
            dma, dma,
            dma, dma,
            dma, dma,
            dma, dma((NQ,)),
            dma, dma,
            dma, dma((NQ, 2)),
            dma((2,)), dma((2,)),
            dma((2,)), dma((2,)),
        ],
        compiler_params=pltpu.CompilerParams(
            collective_id=0, has_side_effects=True, vmem_limit_bytes=56 * 2**20
        ),
        name="subspace",
    )(embeddings, start_vectors)
    return (vectors, degrees.reshape(OWN))


def solution(mesh):
    return jax.shard_map(
        local,
        mesh=mesh,
        in_specs=(P(("row", "col"), None), P(None, ("row", "col"))),
        out_specs=(P(None, ("row", "col")), P(("row", "col"))),
        check_vma=False,
    )
```

```python
import math

import jax
import jax.numpy as jnp
from jax import lax
from jax.experimental import pallas as pl
from jax.experimental.pallas import tpu as pltpu
from jax.sharding import PartitionSpec as P

K = 32
PLACES = ((0, 0), (0, 1), (1, 0), (3, 0), (2, 0), (1, 1), (3, 1), (2, 1))
E = 256
OWN = 320
PAD = 384
NZ = 8
NQ = 4
J = NZ * OWN
PAIR = 2 * OWN
WIDE = NQ * OWN
RATE = 8.0 / math.log(2.0)
MESH = pl.DeviceIdType.MESH
HIGH = lax.Precision.HIGHEST
F32 = jnp.float32
BF16 = jnp.bfloat16


def dot_nt(a, b, precision=None):
    return lax.dot_general(a, b, (((1,), (1,)), ((), ())), precision=precision, preferred_element_type=F32)


def pack(square):
    return jnp.concatenate([square[8 * b : 8 * b + 8, :] for b in range(4)], axis=1)


def unpack(packed):
    return jnp.concatenate([packed[:, K * b : K * b + K] for b in range(4)], axis=0)


def fold(wide):
    n = wide.shape[0]
    rest = [wide[n // 4 * b : n // 4 * (b + 1), 256:OWN] for b in range(4)]
    return jnp.concatenate([wide[:, 0:256], jnp.concatenate(rest, axis=1)], axis=0)


def unfold(folded):
    n = folded.shape[0] // 5 * 4
    rest = [folded[n:, 64 * b : 64 * (b + 1)] for b in range(4)]
    return jnp.concatenate([folded[0:n], jnp.concatenate(rest, axis=0)], axis=1)


def inverse_factor(gram):
    shape = (8, 2 * K)
    ranks = lax.broadcasted_iota(jnp.int32, (8, K), 0)
    lanes = lax.broadcasted_iota(jnp.int32, (8, K), 1)
    rank = lax.broadcasted_iota(jnp.int32, shape, 0)
    work = [
        jnp.concatenate([gram[8 * b : 8 * b + 8], (lanes == ranks + 8 * b).astype(F32)], axis=1) for b in range(4)
    ]
    done = []
    for b in range(4):
        rows = [jnp.broadcast_to(work[b][i : i + 1], shape) for i in range(8)]
        columns = [
            [jnp.broadcast_to(work[c][:, 8 * b + i : 8 * b + i + 1], shape) for c in range(b, 4)] for i in range(8)
        ]
        corner = [[jnp.broadcast_to(columns[j][0][i : i + 1], shape) for j in range(i + 1)] for i in range(8)]
        pivots = corner[0][0]
        for i in range(8):
            pivots = jnp.where(rank == i, corner[i][i], pivots)
            inverse = 1.0 / corner[i][i]
            factors = [column * inverse for column in columns[i]]
            factors[0] = jnp.where(rank > i, factors[0], 0.0)
            for j in range(i + 1, 8):
                factor = corner[j][i] * inverse
                rows[j] = rows[j] - factor * rows[i]
                columns[j] = [old - own * corner[j][i] for old, own in zip(columns[j], factors)]
                for k in range(i + 1, j + 1):
                    corner[j][k] = corner[j][k] - factor * corner[k][i]
            for c in range(b, 4):
                work[c] = work[c] - factors[c - b] * rows[i]
        done.append(work[b] * (1.0 / jnp.sqrt(pivots)))
    return jnp.concatenate(done, axis=0)[:, K : 2 * K]


def kernel(
    emb_ref, start_ref, vec_ref, deg_ref,
    u_i, u_j, tiles, acc, start_all, part, scale_all, lhs, lhs_pair, out_acc,
    send, recv, own_ref, sib_send, sib_recv, sum_send, sum_recv, raw_all, gram_c, gram_r,
    s_i, r_i, s_j, r_j, s_st, r_st, s_pt, r_pt, s_1, r_1, s_sb, r_sb, s_sm, r_sm, s_rw, r_rw, s_gc, r_gc, s_gr, r_gr,
):
    row = lax.axis_index("row")
    col = lax.axis_index("col")
    z, core = row // 2, row % 2
    x, y = col % NQ, col // NQ
    y_rows = y + 1 - 2 * (y % 2)
    y_cols = NQ - 1 - y
    sibling = (z * 2 + 1 - core, col)

    def at_r(dx, dy, dc=0):
        place = (y_rows if dy else y) * NQ + lax.rem(x + dx + NQ, NQ)
        return (z * 2 + (1 - core if dc else core), place)

    def at_c(dz, dy):
        return (lax.rem(z + dz + NQ, NQ) * 2 + core, (y_cols if dy else y) * NQ + x)

    def j_slot(dz, dy):
        return lax.rem(z - dz + NQ, NQ) * 2 + (y // 2) + dy * (1 - 2 * (y // 2))

    offsets_c = [(dz, dy) for dz, dy in PLACES if dz or dy]
    offsets_r = [(dx, dy, dc) for dx, dy in PLACES for dc in range(2) if dx or dy or dc]
    mine = j_slot(0, 0)

    def push(src, dst, s_sem, r_sem, device):
        pltpu.make_async_remote_copy(
            src_ref=src, dst_ref=dst, send_sem=s_sem, recv_sem=r_sem, device_id=device, device_id_type=MESH
        ).start()

    def arrived(ref, r_sem):
        pltpu.make_async_remote_copy(
            src_ref=ref, dst_ref=ref, send_sem=r_sem, recv_sem=r_sem, device_id=sibling, device_id_type=MESH
        ).wait_recv()

    def sent(ref, s_sem):
        pltpu.make_async_remote_copy(
            src_ref=ref, dst_ref=ref, send_sem=s_sem, recv_sem=s_sem, device_id=sibling, device_id_type=MESH
        ).wait_send()

    barrier = pltpu.get_barrier_semaphore()
    neighbours = [at(*place) for at in (at_r, at_c) for place in PLACES[1:5]] + [sibling]
    for device in neighbours:
        pl.semaphore_signal(barrier, inc=1, device_id=device, device_id_type=MESH)

    values = emb_ref[...].astype(F32)
    power = jnp.mean(values * values, axis=1, keepdims=True)
    unit = (values * lax.rsqrt(power + 1e-06) * (1.0 / math.sqrt(E))).astype(BF16)
    u_i[0] = unit
    u_j[mine] = unit
    start_all[mine, :, 0:OWN] = start_ref[...].astype(BF16)
    acc[...] = jnp.zeros_like(acc)
    pl.semaphore_wait(barrier, len(neighbours))

    def i_slot(dx, dy, dc=0):
        return 2 * PLACES.index((dx % NQ, dy)) + dc

    def row_piece(dx, dy, step, flip):
        to = i_slot(dx + step, dy ^ flip)
        push(u_i.at[i_slot(dx, dy)], u_i.at[to], s_i, r_i.at[to], at_r(step, flip))

    def row_over(dx, dy):
        push(u_i.at[i_slot(dx, dy)], u_i.at[i_slot(dx, dy, 1)], s_i, r_i.at[i_slot(dx, dy, 1)], sibling)

    def row_here(dx, dy, dc=0):
        arrived(u_i.at[i_slot(dx, dy, dc)], r_i.at[i_slot(dx, dy, dc)])

    def col_piece(dz, dy, step, flip):
        slot = j_slot(dz, dy)
        push(u_j.at[slot], u_j.at[slot], s_j, r_j.at[(dz + step) % NQ, dy ^ flip], at_c(step, flip))

    def col_here(dz, dy):
        arrived(u_j.at[j_slot(dz, dy)], r_j.at[dz, dy])

    def onward(piece, d, dy):
        if (d, dy) == (0, 1):

            @pl.when(core == 0)
            def _():
                for step in (1, 3, 2):
                    piece(0, 1, step, 0)

        elif dy == 0:
            pl.when(core == 1)(lambda: piece(d, 0, 0, 1))

    def on_row(dx, dy):
        row_here(dx, dy)
        onward(row_piece, dx, dy)
        row_over(dx, dy)

    def on_col(dz, dy):
        col_here(dz, dy)
        onward(col_piece, dz, dy)

    def tile(chunk, slot, low=0, high=WIDE):
        rows_j = pl.ds(pl.multiple_of(slot * OWN, OWN), OWN)
        block = u_i[NQ * chunk + low // OWN : NQ * chunk + high // OWN].reshape(high - low, E)
        value = jnp.exp2(dot_nt(u_j[slot], block) * RATE)
        tiles[chunk, rows_j, low:high] = value.astype(BF16)
        total = acc[rows_j, :]
        for lane in range(0, high - low, 128):
            total = total + value[:, lane : lane + 128]
        acc[rows_j, :] = total

    def tile_range(first, last, places, low=0, high=WIDE):
        for dz, dy in places:
            for chunk in range(first, last):
                tile(chunk, j_slot(dz, dy), low, high)

    near, beside = PLACES[0:4], PLACES[5:7]

    row_over(0, 0)
    for step, flip in ((0, 1), (1, 0), (3, 0), (2, 0)):
        row_piece(0, 0, step, flip)
        col_piece(0, 0, step, flip)
    for place in PLACES[1:4]:
        on_row(*place)
        on_col(*place)
    row_here(0, 0, 1)
    row_here(0, 1, 1)
    tile_range(0, 1, near)
    row_here(1, 0, 1)
    row_here(3, 0, 1)
    tile_range(1, 2, near[0:2])
    on_row(2, 0)
    on_col(2, 0)
    tile_range(1, 2, near[2:4])
    tile_range(0, 2, PLACES[4:5])
    for place in PLACES[5:7]:
        on_row(*place)
        on_col(*place)
    tile_range(0, 2, beside)
    row_here(2, 0, 1)
    row_here(1, 1, 1)
    tile_range(2, 3, PLACES[0:7])
    row_here(3, 1, 1)
    tile_range(3, 4, PLACES[0:7], 0, PAIR)
    on_row(2, 1)
    on_col(2, 1)
    for dz, dy in offsets_c:
        push(start_all.at[mine], start_all.at[mine], s_st, r_st, at_c(dz, dy))
    tile_range(0, 3, PLACES[7:8])
    tile_range(3, 4, PLACES[7:8], 0, PAIR)
    row_here(2, 1, 1)
    tile_range(3, 4, PLACES, PAIR, WIDE)

    ones = jnp.ones((8, 128), BF16)
    for slot in range(NZ):
        left = acc[slot * OWN : (slot + 1) * OWN, :]
        total = jnp.zeros((8, OWN), F32)
        for _ in range(2):
            top = left.astype(BF16)
            left = left - top.astype(F32)
            total = total + dot_nt(ones, top)
        part[0, slot : slot + 1, 0:OWN] = total[0:1, :]
    for n, (dz, dy) in enumerate(offsets_c):
        push(part.at[0], part.at[n + 1], s_pt, r_pt, at_c(dz, dy))
    arrived(part.at[1:8], r_pt)
    degrees = part[0, :, 0:OWN]
    for n in range(1, NZ):
        degrees = degrees + part[n, :, 0:OWN]
    scales = 1.0 / jnp.sqrt(degrees)
    scale_all[0] = scales
    scale_all[1] = degrees * math.exp(-8.0)
    deg_ref[...] = scale_all[1, pl.ds(mine, 1), :]
    scale = scale_all[0, pl.ds(mine, 1), :]
    arrived(start_all.at[0:7], r_st)
    for slot in range(NZ):
        lhs[:, slot * OWN : (slot + 1) * OWN] = (start_all[slot, :, 0:OWN].astype(F32) * scales[slot : slot + 1, :]).astype(BF16)

    for chunk in (3, 2, 1, 0):
        out = jnp.dot(lhs[...], tiles[chunk], preferred_element_type=F32)
        for sub in range(NQ):
            slot = NQ * chunk + sub
            block = out[:, sub * OWN : (sub + 1) * OWN]
            if slot == 0:
                own_ref[...] = block
            else:
                dx, dy = PLACES[slot // 2]
                send[slot, :, 0:OWN] = block.astype(BF16)
                push(send.at[slot], recv.at[slot], s_1, r_1, at_r(-dx, dy, slot % 2))
    arrived(recv.at[1:16], r_1)
    image = own_ref[...]
    for slot in range(1, 2 * NZ):
        image = image + recv[slot, :, 0:OWN].astype(F32)
    image = image * scale

    raw = image * scale
    high = raw.astype(BF16)
    raw_all[mine] = fold(jnp.concatenate([high, (raw - high.astype(F32)).astype(BF16)], axis=0))
    for dz, dy in ((0, 1), (1, 0), (3, 0), (1, 1), (3, 1), (2, 0), (2, 1)):
        push(raw_all.at[mine], raw_all.at[mine], s_rw, r_rw.at[dz, dy], at_c(dz, dy))

    def gram_start(step, image):
        gram_c[step, 0] = pack(dot_nt(image, image, HIGH))
        for n, (dz, dy) in enumerate(offsets_c):
            push(gram_c.at[step, 0], gram_c.at[step, n + 1], s_gc.at[step], r_gc.at[step], at_c(dz, dy))

    def gram_middle(step):
        arrived(gram_c.at[step, 1:8], r_gc.at[step])
        gram = gram_c[step, 0]
        for n in range(1, NZ):
            gram = gram + gram_c[step, n]
        gram_r[step, 0] = gram
        for n, (dx, dy, dc) in enumerate(offsets_r):
            push(gram_r.at[step, 0], gram_r.at[step, n + 1], s_gr.at[step], r_gr.at[step], at_r(dx, dy, dc))

    def gram_end(step):
        arrived(gram_r.at[step, 1:16], r_gr.at[step])
        gram = gram_r[step, 0]
        for n in range(1, 2 * NZ):
            gram = gram + gram_r[step, n]
        return inverse_factor(unpack(gram))

    gram_start(0, image)

    def to_sibling(chunk, out):
        pair = pl.ds(2 * chunk, 2)
        for sub in range(2):
            sum_send[2 * chunk + sub] = fold(out[:, sub * PAIR : sub * PAIR + OWN])
            sib_send[2 * chunk + sub] = fold(out[:, sub * PAIR + OWN : (sub + 1) * PAIR])
        push(sib_send.at[pair], sib_recv.at[pair], s_sb, r_sb.at[chunk], sibling)

    def to_owners(chunk):
        arrived(sib_recv.at[pl.ds(2 * chunk, 2)], r_sb.at[chunk])
        for n in (2 * chunk + 1, 2 * chunk):
            dx, dy = PLACES[n]
            sum_send[n] += sib_recv[n]
            if n:
                push(sum_send.at[n], sum_recv.at[n], s_sm, r_sm, at_r(-dx, dy))

    def product(dz, chunk):
        rows = pl.ds(pl.multiple_of(lax.rem(z - dz + NQ, NQ) * PAIR, PAIR), PAIR)
        out = jnp.dot(lhs_pair[dz], tiles[chunk, rows, :], preferred_element_type=F32)
        return out[0:K] + out[K : 2 * K]

    def ready(dz):
        first = lax.rem(z - dz + NQ, NQ) * 2
        for dy in range(2):
            if dz or dy:
                arrived(raw_all.at[j_slot(dz, dy)], r_rw.at[dz, dy])
        lhs_pair[dz, :, 0:OWN] = unfold(raw_all[first])
        lhs_pair[dz, :, OWN:PAIR] = unfold(raw_all[first + 1])

    ready(0)
    for chunk in range(4):
        out_acc[chunk] = product(0, chunk)
    ready(1)
    ready(3)
    for chunk in range(4):
        out_acc[chunk] += product(1, chunk) + product(3, chunk)
    gram_middle(0)
    ready(2)
    for chunk in (3, 2, 1, 0):
        to_sibling(chunk, out_acc[chunk] + product(2, chunk))
        if chunk < 3:
            to_owners(chunk + 1)
    to_owners(0)
    inverse = gram_end(0)
    arrived(sum_recv.at[1:8], r_sm)
    total = sum_send[0]
    for n in range(1, NZ):
        total = total + sum_recv[n]
    image = unfold(total) * scale
    image = jnp.dot(inverse, image, precision=HIGH, preferred_element_type=F32)
    gram_start(1, image)
    gram_middle(1)
    inverse = gram_end(1)
    vec_ref[...] = jnp.dot(inverse, image, precision=HIGH, preferred_element_type=F32)

    sent(u_i.at[0:15], s_i)
    sent(u_j.at[0:7], s_j)
    sent(start_all.at[0:7], s_st)
    sent(part.at[1:8], s_pt)
    sent(raw_all.at[0:7], s_rw)
    sent(send.at[1:16], s_1)
    sent(sib_send, s_sb)
    sent(sum_send.at[1:8], s_sm)
    for step in range(2):
        sent(gram_c.at[step, 1:8], s_gc.at[step])
        sent(gram_r.at[step, 1:16], s_gr.at[step])


def local(embeddings, start_vectors):
    dma = pltpu.SemaphoreType.DMA
    vmem = pltpu.VMEM
    vectors, degrees = pl.pallas_call(
        kernel,
        out_shape=(vmem((K, OWN), F32), vmem((1, OWN), F32)),
        in_specs=[pl.BlockSpec(memory_space=vmem)] * 2,
        out_specs=(pl.BlockSpec(memory_space=vmem), pl.BlockSpec(memory_space=vmem)),
        scratch_shapes=[
            vmem((NQ * NQ, OWN, E), BF16),
            vmem((NZ, OWN, E), BF16),
            vmem((NQ, J, WIDE), BF16),
            vmem((J, 128), F32),
            vmem((NZ, K, PAD), BF16),
            vmem((NZ, NZ, PAD), F32),
            vmem((2, NZ, OWN), F32),
            vmem((K, J), BF16),
            vmem((NQ, 2 * K, PAIR), BF16),
            vmem((NQ, K, WIDE), F32),
            vmem((2 * NZ, K, PAD), BF16),
            vmem((2 * NZ, K, PAD), BF16),
            vmem((K, OWN), F32),
            vmem((NZ, K + K // 4, 256), F32),
            vmem((NZ, K + K // 4, 256), F32),
            vmem((NZ, K + K // 4, 256), F32),
            vmem((NZ, K + K // 4, 256), F32),
            vmem((NZ, 2 * K + K // 2, 256), BF16),
            vmem((2, NZ, 8, 128), F32),
            vmem((2, 2 * NZ, 8, 128), F32),
            dma, dma((2 * NZ,)),
            dma, dma((NQ, 2)),
            dma, dma,
            dma, dma,
            dma, dma,
            dma, dma((NQ,)),
            dma, dma,
            dma, dma((NQ, 2)),
            dma((2,)), dma((2,)),
            dma((2,)), dma((2,)),
        ],
        compiler_params=pltpu.CompilerParams(
            collective_id=0, has_side_effects=True, vmem_limit_bytes=56 * 2**20
        ),
        name="subspace",
    )(embeddings, start_vectors)
    return (vectors, degrees.reshape(OWN))


def solution(mesh):
    return jax.shard_map(
        local,
        mesh=mesh,
        in_specs=(P(("row", "col"), None), P(None, ("row", "col"))),
        out_specs=(P(None, ("row", "col")), P(("row", "col"))),
        check_vma=False,
    )
```
